256 devices in a mesh: dap: 128 (over x_lo, y, z, core), dp: 2 (over x_hi).
Axes of the slice: x: 4 (x_hi: 2, x_lo: 2; x = x_hi * 2 + x_lo), y: 4, z: 8, core: 2. Of those that a mesh axis runs over, the one named last changes fastest.
Arguments:
- aligned_rows: bfloat16 [256, 512, 256], P(('dp', 'dap')), parts along dimension 0, may hold values from -6 to 6
- asking_projection: bfloat16 [256, 256], replicated, may hold values from -1.5 to 1.5
- lookup_projection: bfloat16 [256, 256], replicated, may hold values from -0.25 to 0.25
- content_projection: bfloat16 [256, 256], replicated, may hold values from -0.375 to 0.375
- sigmoid_projection: bfloat16 [256, 256], replicated, may hold values from -0.375 to 0.375
- sigmoid_shift: float32 [256], replicated, may hold values from -2 to 2
- result_projection: bfloat16 [256, 256], replicated, may hold values from -0.375 to 0.375
- tensor_mean_projections: bfloat16 [256, 64], replicated, may hold values from -0.375 to 0.375
- twofold_projection: bfloat16 [1024, 128], replicated, may hold values from -0.1875 to 0.1875
- refreshed_rows_adjoint: bfloat16 [256, 512, 256], P(('dp', 'dap')), parts along dimension 0, may hold values from -6 to 6
- twofold_change_adjoint: bfloat16 [1024, 512, 128], P(('dp', 'dap')), parts along dimension 0, may hold values from -96 to 96
Outputs:
- entering_rows_derivative: bfloat16 [256, 512, 256], P(('dp', 'dap')), parts along dimension 0
- pair_weight_grad: float32 [2048, 128], P('dp'), parts along dimension 0
- outer_weight_grad: float32 [512, 64], P('dp'), parts along dimension 0
- right_factor_grad: float32 [256, 512, 32], P('dp', 'dap'), parts along dimension 0
The draws below stay inside these ranges and needn't reach their ends.
There are 2 independent parts, one for each index of `dp`. The reference program is written for one: setup_inputs(seed, part) draws one part's arguments, and reference() takes and returns one part's arrays. A program takes and returns all parts, laid end to end along the dimension named above; an argument that names none is the same for every part. Nothing has to cross between parts.
All inputs are finite; a program needn't handle non-finite values.
Results may differ from the reference program's by a relative error of at most 0.035.
Values may be sent and summed in bfloat16 or wider, within the bound.
A program may use at most 128 MiB of HBM per device.

```python
import jax
import jax.numpy as jnp
from jax import lax

ROW_FEATURES = 256
CZ = 128
NUM_ATTENDERS = 8
PER_HEAD_DIM = 32
FACTOR_DIM = 32
SHARD_POSITIONS = 4
NUM_ALIGNED = 128
NUM_POSITIONS = 512
N_DAP = 128


def shared_matrix(key):
    return jax.random.truncated_normal(key, -4.0, 4.0, (ROW_FEATURES, NUM_ATTENDERS * PER_HEAD_DIM), jnp.float32) / jnp.sqrt(jnp.float32(ROW_FEATURES))


def draw_lookup_projection(key, part):
    base = shared_matrix(key)
    return base.astype(jnp.bfloat16)


def draw_asking_projection(key, part):
    key = jax.random.fold_in(key, 7)
    own_part = shared_matrix(key)
    return own_part.astype(jnp.bfloat16)


def spiked(drawn, own_key, source, target, shards_of, factor):
    owner, partner = [(jnp.arange(drawn.shape[dim]) // (drawn.shape[dim] // shards_of)).reshape([-1 if axis == dim else 1 for axis in range(drawn.ndim)]) for dim in (source, target)]
    chosen = jax.random.permutation(own_key, shards_of)[partner]
    strong = (owner == chosen) | (owner == (partner + shards_of // 2) % shards_of)
    return jnp.where(strong, factor * drawn, drawn)


def levels(rng, dims, pieces, smallest, high):
    def one(axis_at, shards_of):
        draws = jax.random.uniform(jax.random.fold_in(jax.random.fold_in(rng, 6), axis_at), (shards_of,), jnp.float32, smallest / len(pieces), high / len(pieces))
        return jnp.repeat(jnp.exp(draws), dims[axis_at] // shards_of).reshape((-1,) + (1,) * (len(dims) - axis_at - 1))

    factor_of = one(*pieces[0])
    for cut in pieces[1:]:
        factor_of = factor_of * one(*cut)
    return factor_of


def scatter_about(rng, shape, width, limit, split=(), kind=jnp.bfloat16):
    gain = levels(rng, shape, split, -0.22, 0.18) if split else 1.0
    drawn = jax.random.normal(rng, shape, jnp.float32) * width * gain
    return jnp.minimum(jnp.maximum(drawn, -limit), limit).astype(kind)


def gaussian_with(key, shape, deviation, most, split, heavy, kind=jnp.bfloat16):
    drawn = deviation * jax.random.normal(key, shape, jnp.float32)
    if split:
        drawn = drawn * levels(key, shape, split, -0.22, 0.18)
    return jnp.clip(spiked(drawn, jax.random.fold_in(key, 3), *heavy), -most, most).astype(kind)


def setup_inputs(seed: int = 0, part: int = 0) -> dict:
    splits = jax.random.split(jax.random.key(seed), 12)
    part_keys = jax.random.split(jax.random.fold_in(splits[11], part), 12)
    return {
        "aligned_rows": scatter_about(part_keys[0], (NUM_ALIGNED, NUM_POSITIONS, ROW_FEATURES), 1.0, 6.0, ((0, 128),)),
        "asking_projection": draw_asking_projection(jax.random.fold_in(splits[11], 71), part),
        "lookup_projection": draw_lookup_projection(jax.random.fold_in(splits[11], 71), part),
        "content_projection": scatter_about(splits[3], (ROW_FEATURES, NUM_ATTENDERS * PER_HEAD_DIM), ROW_FEATURES ** -0.5, 0.375),
        "sigmoid_projection": scatter_about(splits[4], (ROW_FEATURES, NUM_ATTENDERS * PER_HEAD_DIM), ROW_FEATURES ** -0.5, 0.375),
        "sigmoid_shift": jnp.clip(jax.random.uniform(splits[5], (NUM_ATTENDERS * PER_HEAD_DIM,), jnp.float32, -2.0, 2.0), -2.0, 2.0),
        "result_projection": scatter_about(splits[6], (NUM_ATTENDERS * PER_HEAD_DIM, ROW_FEATURES), (NUM_ATTENDERS * PER_HEAD_DIM) ** -0.5, 0.375),
        "tensor_mean_projections": scatter_about(splits[7], (ROW_FEATURES, 2 * FACTOR_DIM), ROW_FEATURES ** -0.5, 0.375),
        "twofold_projection": scatter_about(splits[8], (FACTOR_DIM * FACTOR_DIM, CZ), (FACTOR_DIM * FACTOR_DIM) ** -0.5, 0.1875),
        "refreshed_rows_adjoint": scatter_about(part_keys[9], (NUM_ALIGNED, NUM_POSITIONS, ROW_FEATURES), 1.0, 6.0, ((0, 128),)),
        "twofold_change_adjoint": gaussian_with(part_keys[10], (NUM_POSITIONS, NUM_POSITIONS, CZ), 4.0, 96.0, ((0, 128),), (0, 1, 128, 5.5)),
    }


def layer_standardize(values):
    wide = values.astype(jnp.float32)
    average = lax.optimization_barrier(jnp.mean(wide, axis=-1, keepdims=True))
    centred = wide - average
    variance = lax.optimization_barrier(jnp.mean(centred * centred, axis=-1, keepdims=True))
    return (centred * lax.rsqrt(variance + 1e-05)).astype(jnp.bfloat16)

def column_self_attention(alignment_block, asking_projection, lookup_projection, content_projection, sigmoid_projection, sigmoid_shift, result_projection):
    sequence_total, residue_total, channel_width = alignment_block.shape
    normalised_rows = layer_standardize(alignment_block).reshape(sequence_total * residue_total, channel_width)

    def project(weight):
        return jnp.dot(normalised_rows, weight, preferred_element_type=jnp.float32)
    head_shape = (sequence_total, residue_total, NUM_ATTENDERS, PER_HEAD_DIM)
    query_heads = (project(asking_projection) * PER_HEAD_DIM ** (-0.5)).astype(jnp.bfloat16).reshape(head_shape)
    key_heads = project(lookup_projection).astype(jnp.bfloat16).reshape(head_shape)
    value_heads = project(content_projection).astype(jnp.bfloat16).reshape(head_shape)
    gating = jax.nn.sigmoid(project(sigmoid_projection) + sigmoid_shift)
    scores = jnp.einsum('schd,tchd->chst', query_heads.astype(jnp.float32), key_heads.astype(jnp.float32))
    weights = jax.nn.softmax(scores, axis=-1).astype(jnp.bfloat16)
    attended = jnp.einsum('chst,tchd->schd', weights.astype(jnp.float32), value_heads.astype(jnp.float32))
    gated = (attended.reshape(sequence_total * residue_total, NUM_ATTENDERS * PER_HEAD_DIM) * gating).astype(jnp.bfloat16)
    return jnp.dot(gated, result_projection, preferred_element_type=jnp.float32).reshape(sequence_total, residue_total, channel_width)

def reference(aligned_rows, asking_projection, lookup_projection, content_projection, sigmoid_projection, sigmoid_shift, result_projection, tensor_mean_projections, twofold_projection, refreshed_rows_adjoint, twofold_change_adjoint):
    arriving_pieces = aligned_rows.reshape(NUM_ALIGNED, N_DAP, SHARD_POSITIONS, ROW_FEATURES).transpose(1, 0, 2, 3)
    adjoint_pieces = refreshed_rows_adjoint.reshape(NUM_ALIGNED, N_DAP, SHARD_POSITIONS, ROW_FEATURES).transpose(1, 0, 2, 3)

    def apply_column_heads(alignment_block):
        return column_self_attention(alignment_block, asking_projection, lookup_projection, content_projection, sigmoid_projection, sigmoid_shift, result_projection)

    def block_forward_pass(alignment_block):
        updated_alignment = (alignment_block.astype(jnp.float32) + apply_column_heads(alignment_block)).astype(jnp.bfloat16)
        normalised_rows = layer_standardize(updated_alignment)
        projected_halves = jnp.dot(normalised_rows.reshape(-1, ROW_FEATURES), tensor_mean_projections, preferred_element_type=jnp.float32)
        return (updated_alignment, projected_halves.astype(jnp.bfloat16).reshape(NUM_ALIGNED, SHARD_POSITIONS, 2 * FACTOR_DIM))
    refreshed_everything, factor_all = lax.map(block_forward_pass, arriving_pieces)
    right_whole = factor_all[..., FACTOR_DIM:].transpose(1, 0, 2, 3).reshape(NUM_ALIGNED, NUM_POSITIONS, FACTOR_DIM)
    pair_blocks = twofold_change_adjoint.reshape(N_DAP, SHARD_POSITIONS, NUM_POSITIONS, CZ)

    def pair_step(running_state, input_arrays):
        pair_update_gradient, grad_right = running_state
        left_factor, pair_rows = input_arrays
        outer = (jnp.einsum('sic,sje->ijce', left_factor.astype(jnp.float32), right_whole.astype(jnp.float32)) / NUM_ALIGNED).astype(jnp.bfloat16)
        flat_rows = pair_rows.reshape(-1, CZ)
        pair_grad = (jnp.dot(flat_rows, twofold_projection.T, preferred_element_type=jnp.float32) / NUM_ALIGNED).astype(jnp.bfloat16).reshape(SHARD_POSITIONS, NUM_POSITIONS, FACTOR_DIM, FACTOR_DIM)
        pair_update_gradient = pair_update_gradient + jnp.dot(outer.reshape(-1, FACTOR_DIM * FACTOR_DIM).T, flat_rows, preferred_element_type=jnp.float32)
        first_half_derivative = jnp.einsum('ijce,sje->sic', pair_grad.astype(jnp.float32), right_whole.astype(jnp.float32)).astype(jnp.bfloat16)
        grad_right = grad_right + jnp.einsum('sic,ijce->sje', left_factor.astype(jnp.float32), pair_grad.astype(jnp.float32))
        return ((pair_update_gradient, grad_right), first_half_derivative)
    start_carry = (jnp.zeros((FACTOR_DIM * FACTOR_DIM, CZ), jnp.float32), jnp.zeros((NUM_ALIGNED, NUM_POSITIONS, FACTOR_DIM), jnp.float32))
    (pair_update_gradient, grad_right), first_half_derivative = lax.scan(pair_step, start_carry, (factor_all[..., :FACTOR_DIM], pair_blocks))
    second_half_pieces = grad_right.astype(jnp.bfloat16).reshape(NUM_ALIGNED, N_DAP, SHARD_POSITIONS, FACTOR_DIM).transpose(1, 0, 2, 3)

    def reverse_sweep_body(running_state, input_arrays):
        alignment_block, updated_alignment, output_cotangent, left_factor_gradient, right_factor_gradient = input_arrays
        normalised_rows, norm_vjp = jax.vjp(layer_standardize, updated_alignment)
        halves_derivative = jnp.concatenate([left_factor_gradient, right_factor_gradient], axis=-1).reshape(-1, 2 * FACTOR_DIM)
        running_state = running_state + jnp.dot(normalised_rows.reshape(-1, ROW_FEATURES).T, halves_derivative, preferred_element_type=jnp.float32)
        normalised_derivative = jnp.dot(halves_derivative, tensor_mean_projections.T, preferred_element_type=jnp.float32).astype(jnp.bfloat16).reshape(NUM_ALIGNED, SHARD_POSITIONS, ROW_FEATURES)
        grad_updated, = norm_vjp(normalised_derivative)
        grad_mid = (output_cotangent.astype(jnp.float32) + grad_updated.astype(jnp.float32)).astype(jnp.bfloat16)
        ignored_value, attention_pullback = jax.vjp(apply_column_heads, alignment_block)
        grad_attn, = attention_pullback(grad_mid.astype(jnp.float32))
        return (running_state, (grad_mid.astype(jnp.float32) + grad_attn.astype(jnp.float32)).astype(jnp.bfloat16))
    tensor_mean_derivative, parameter_derivatives = lax.scan(reverse_sweep_body, jnp.zeros((ROW_FEATURES, 2 * FACTOR_DIM), jnp.float32), (arriving_pieces, refreshed_everything, adjoint_pieces, first_half_derivative, second_half_pieces))
    entering_rows_derivative = parameter_derivatives.transpose(1, 0, 2, 3).reshape(NUM_ALIGNED, NUM_POSITIONS, ROW_FEATURES)
    return (entering_rows_derivative, pair_update_gradient, tensor_mean_derivative, grad_right)
```

```python
import functools

import jax
import jax.numpy as jnp
from jax import lax
from jax.experimental import pallas as pl
from jax.experimental.pallas import tpu as pltpu
from jax.sharding import PartitionSpec as P

HEADS = 8
HEAD_DIM = 32
SEQ = 128
RES = 4
CH = 256
N_DAP = 128
N_WIDE = 16
N_Z = 8
MESH = pl.DeviceIdType.MESH
F32 = jnp.float32
BF16 = jnp.bfloat16


def nn(a, b):
    return lax.dot_general(a, b, (((1,), (0,)), ((), ())), preferred_element_type=F32)


def nt(a, b):
    return lax.dot_general(a, b, (((1,), (1,)), ((), ())), preferred_element_type=F32)


def peer_all(me, k):
    return lax.rem(me + k, N_DAP)


def peer_z(me, k):
    low = lax.rem(me, 16)
    return me - low + lax.rem(low + 2 * k, 16)


def peer_wide(me, k):
    core = lax.rem(me, 2)
    member = lax.rem((me // 16) * 2 + core + k, N_WIDE)
    return (member // 2) * 16 + lax.rem(me, 16) - core + lax.rem(member, 2)


def place_wide(me):
    return (me // 16) * 2 + lax.rem(me, 2)


def place_z(me):
    return lax.rem(me, 16) // 2


def push(peer_of, place_of, total, me, src, dst, send_sem, recv_sem, spread):
    mine = place_of(me)

    def one(k, carry):
        peer = peer_of(me, k)
        pltpu.make_async_remote_copy(
            src_ref=src.at[place_of(peer)] if spread else src,
            dst_ref=dst.at[mine],
            send_sem=send_sem,
            recv_sem=recv_sem,
            device_id={"dap": peer},
            device_id_type=MESH,
        ).start()
        return carry

    lax.fori_loop(1, total, one, 0)


def drain(ref, total, sem):
    part = ref.at[pl.ds(0, total - 1)]
    pltpu.make_async_copy(part, part, sem).wait()


def standardize(wide):
    average = jnp.mean(wide, axis=-1, keepdims=True)
    centred = wide - average
    variance = jnp.mean(centred * centred, axis=-1, keepdims=True)
    scale = lax.rsqrt(variance + 1e-05)
    return centred * scale, scale


def standardize_back(grad, hat, scale):
    return scale * (
        grad
        - jnp.mean(grad, axis=-1, keepdims=True)
        - hat * jnp.mean(grad * hat, axis=-1, keepdims=True)
    )


def kernel(
    rows_ref, wq_ref, wk_ref, wv_ref, wg_ref, shift_ref, wo_ref, wf_ref, wp_ref, adj_ref, pair_ref,
    out_ref, pwg_ref, owg_ref, rfg_ref,
    xs, xr, us, ur, gs, gr, t32, x32, hat_in, sc_in, gate, att, q_all, k_all, v_all, w_all,
    nmid, hat_mid, sc_mid, fac_t, ls, lg, rs, rg, lp, g2, w2, y, xp, pacc, gls, glr, grs, grr,
    dcat, ps, pr, zs, zr, fs, fr, os, orr, send, recv,
):
    me = lax.axis_index("dap")
    wide = place_wide(me)
    along = place_z(me)
    bar = pltpu.get_barrier_semaphore()

    def greet(k, carry):
        pl.semaphore_signal(bar, inc=1, device_id={"dap": peer_all(me, k)}, device_id_type=MESH)
        return carry

    lax.fori_loop(1, N_DAP, greet, 0)

    def stage_rows(ref, dst):
        t32[pl.ds(0, 512, stride=2), :] = ref[:, 0:128].astype(F32)
        t32[pl.ds(1, 512, stride=2), :] = ref[:, 128:256].astype(F32)
        dst[...] = t32[0:1024, :].reshape(N_DAP, 8, 128).astype(BF16)

    stage_rows(rows_ref, xs)
    g2[...] = jnp.zeros_like(g2)
    fac_t[...] = wf_ref[...].astype(F32).T.astype(BF16)
    for c_hi in range(16):
        for c_lo in range(2):
            w2[c_hi * 32:(c_hi + 1) * 32, c_lo * 128:(c_lo + 1) * 128] = (
                wp_ref[(2 * c_hi + c_lo) * 32:(2 * c_hi + c_lo + 1) * 32, :].astype(F32) * (1.0 / SEQ)
            ).astype(BF16)
    xr[me] = xs[me]
    pl.semaphore_wait(bar, N_DAP - 1)

    push(peer_all, lambda d: d, N_DAP, me, xs, xr, send.at[0], recv.at[0], True)

    t32[...] = pair_ref[...].astype(F32)

    def stage_pair(at, carry):
        for core in range(2):
            for i in range(RES):
                parts = [
                    t32[pl.ds(i * 512 + at * 64 + core * 4 + r, 8, stride=8), :] for r in range(RES)
                ]
                gs[at * 2 + core, i * 32:(i + 1) * 32, :] = jnp.concatenate(parts, axis=0).astype(BF16)
        return carry

    lax.fori_loop(0, 8, stage_pair, 0)
    gr[wide] = gs[wide]
    push(peer_wide, place_wide, N_WIDE, me, gs, gr, send.at[1], recv.at[1], True)
    stage_rows(adj_ref, us)
    ur[me] = us[me]

    drain(xr, N_DAP, recv.at[0])
    push(peer_all, lambda d: d, N_DAP, me, us, ur, send.at[2], recv.at[2], True)

    t32[0:1024, :] = xr[...].astype(F32).reshape(1024, 128)
    lane_head = lax.broadcasted_iota(jnp.int32, (1, CH), 1) // HEAD_DIM
    masks = [(lane_head == h).astype(F32).astype(BF16) for h in range(HEADS)]

    def blocks(value):
        return jnp.concatenate([value * m for m in masks], axis=0)

    def side_by_side(value):
        return jnp.concatenate([value[h * 128:(h + 1) * 128, :] for h in range(HEADS)], axis=1)

    def forward(r, carry):
        x = jnp.concatenate(
            [t32[pl.ds(2 * r + half, SEQ, stride=8), :] for half in range(2)], axis=1
        )
        x32[r] = x
        hat, scale = standardize(x)
        hat_in[r] = hat
        sc_in[r] = jnp.broadcast_to(scale, (SEQ, 128))
        normed = hat.astype(BF16)
        q = (nn(normed, wq_ref[...]) * HEAD_DIM ** (-0.5)).astype(BF16)
        k = nn(normed, wk_ref[...]).astype(BF16)
        v = nn(normed, wv_ref[...]).astype(BF16)
        g = jax.nn.sigmoid(nn(normed, wg_ref[...]) + shift_ref[...])
        q_all[r] = q
        k_all[r] = k
        v_all[r] = v
        gate[r] = g
        scores = nt(blocks(q), k)
        e = jnp.exp(scores - jnp.max(scores, axis=-1, keepdims=True))
        w = e * (1.0 / jnp.sum(e, axis=-1, keepdims=True))
        w_all[r] = w
        a = nn(side_by_side(w.astype(BF16)), blocks(v))
        att[r] = a
        gated = (a * g).astype(BF16)
        upd = (x + nn(gated, wo_ref[...])).astype(BF16).astype(F32)
        hat, scale = standardize(upd)
        hat_mid[r] = hat
        sc_mid[r] = jnp.broadcast_to(scale, (SEQ, 128))
        normed = hat.astype(BF16)
        nmid[r] = normed
        factors = nt(fac_t[...], normed).astype(BF16)
        at = pl.multiple_of(r * 32, 32)
        ls[pl.ds(at, 32), :] = factors[0:32, :]
        rs[pl.ds(at, 32), :] = factors[32:64, :]
        return carry

    lax.fori_loop(0, RES, forward, 0)

    push(peer_z, place_z, N_Z, me, rs, rg, send.at[3], recv.at[3], False)
    push(peer_wide, place_wide, N_WIDE, me, ls, lg, send.at[4], recv.at[4], False)
    rg[along] = rs[...]
    lg[wide] = ls[...]

    drain(gr, N_WIDE, recv.at[1])
    t32[...] = gr[...].astype(F32).reshape(2048, 128)

    def build(jn, carry):
        jp = lax.rem(jn, 4) * 8 + jn // 4
        part = jnp.concatenate(
            [t32[pl.ds(r * 32 + jp, 16, stride=128), :] for r in range(RES)], axis=0
        ).astype(BF16)
        g2[jn, 0:64, 0:128] = part
        g2[jn, 64:128, 128:256] = part
        return carry

    lax.fori_loop(0, 32, build, 0)

    def pair_grad(at, carry):
        res = nt(w2[...], g2[pl.ds(at * 4, 4)].reshape(512, 256)).astype(BF16)
        for jj in range(4):
            for c_hi in range(16):
                y[at * 4 + jj, :, c_hi * 128:(c_hi + 1) * 128] = res[
                    c_hi * 32:(c_hi + 1) * 32, jj * 128:(jj + 1) * 128
                ]
        return carry

    lax.fori_loop(0, 8, pair_grad, 0)

    drain(lg, N_WIDE, recv.at[4])
    t32[...] = lg[...].astype(F32).reshape(2048, 128)

    def order_left(c, carry):
        part = jnp.concatenate(
            [t32[pl.ds(r * 32 + c, 16, stride=128), :] for r in range(RES)], axis=0
        )
        lp[pl.ds(pl.multiple_of(c * 64, 64), 64), :] = part.astype(BF16)
        return carry

    lax.fori_loop(0, 32, order_left, 0)

    def right_grad(at, carry):
        res = nn(y[pl.ds(at * 8, 8)].reshape(256, 2048), lp[...]).astype(BF16)
        grs[pl.ds(at * 2, 2)] = res.reshape(2, 128, 128)
        return carry

    lax.fori_loop(0, 4, right_grad, 0)
    grr[along] = grs[along]
    push(peer_z, place_z, N_Z, me, grs, grr, send.at[5], recv.at[5], True)

    drain(rg, N_Z, recv.at[3])
    rg_t = rg[...].reshape(1024, 128).astype(F32).T.astype(BF16)

    def left_grad(at, carry):
        col = pl.multiple_of(at * 512, 512)
        res = nn(rg_t, y[:, :, pl.ds(col, 512)].reshape(1024, 512))
        t32[pl.ds(col, 512), :] = res.T
        return carry

    lax.fori_loop(0, 4, left_grad, 0)

    def stage_left(m, carry):
        part = jnp.concatenate(
            [t32[pl.ds(m + 16 * r, 32, stride=64), :] for r in range(RES)], axis=0
        )
        gls[m] = part.astype(BF16)
        return carry

    lax.fori_loop(0, 16, stage_left, 0)
    glr[wide] = gls[wide]
    push(peer_wide, place_wide, N_WIDE, me, gls, glr, send.at[6], recv.at[6], True)

    pacc[...] = jnp.zeros_like(pacc)

    def pair_weight(at, carry):
        rows = rg[pl.ds(at * 2, 2)].reshape(256, 128)
        for group in range(4):
            res = nt(rows, lp[group * 512:(group + 1) * 512, :]).astype(BF16)
            for jj in range(8):
                for cc in range(4):
                    c_hi = group * 4 + cc
                    xp[c_hi * 32:(c_hi + 1) * 32, jj * 128:(jj + 1) * 128] = res[
                        jj * 32:(jj + 1) * 32, cc * 128:(cc + 1) * 128
                    ]
        pacc[...] += nn(xp[...], g2[pl.ds(at * 8, 8)].reshape(1024, 256))
        return carry

    lax.fori_loop(0, 4, pair_weight, 0)

    drain(grr, N_Z, recv.at[5])
    right_sum = jnp.sum(grr[...].astype(F32), axis=0)
    drain(glr, N_WIDE, recv.at[6])
    left_sum = jnp.sum(glr[...].astype(F32), axis=0)
    rfg_ref[...] = right_sum.T
    owg = jnp.zeros((64, CH), F32)
    for r in range(RES):
        both = jnp.concatenate(
            [left_sum[r * 32:(r + 1) * 32, :], right_sum[r * 32:(r + 1) * 32, :]], axis=0
        )
        owg = owg + nn(both.astype(BF16), nmid[r])
        dcat[r] = both.T.astype(BF16)

    for m in range(16):
        part = pacc[m * 32:(m + 1) * 32, :] * (1.0 / SEQ)
        half = m // 8
        ps[m] = jnp.concatenate(
            [
                part[:, 0:128],
                part[:, 128:256],
                owg[(m % 8) * 8:(m % 8) * 8 + 8, half * 128:(half + 1) * 128],
                jnp.zeros((8, 128), F32),
            ],
            axis=0,
        ).astype(BF16)
    pr[wide] = ps[wide]
    push(peer_wide, place_wide, N_WIDE, me, ps, pr, send.at[7], recv.at[7], True)

    drain(ur, N_DAP, recv.at[2])
    t32[1024:2048, :] = ur[...].astype(F32).reshape(1024, 128)

    def backward(r, carry):
        grad = nn(dcat[r], fac_t[...]).astype(BF16).astype(F32)
        dmid = standardize_back(grad, hat_mid[r], sc_mid[r][:, 0:1]).astype(BF16).astype(F32)
        arriving = jnp.concatenate(
            [t32[pl.ds(1024 + 2 * r + half, SEQ, stride=8), :] for half in range(2)], axis=1
        )
        gm16 = (arriving + dmid).astype(BF16)
        gm = gm16.astype(F32)
        dgated = nt(gm16, wo_ref[...]).astype(BF16).astype(F32)
        g = gate[r]
        datt = blocks((dgated * g).astype(BF16))
        dpre = (dgated * att[r] * g * (1.0 - g)).astype(BF16)
        w = w_all[r]
        dw = nt(datt, v_all[r])
        ds = w * (dw - jnp.sum(w * dw, axis=-1, keepdims=True))
        dq = nn(side_by_side(ds.astype(BF16)), blocks(k_all[r])).astype(BF16)
        dq = (dq.astype(F32) * HEAD_DIM ** (-0.5)).astype(BF16)
        dk = nn(ds.T.astype(BF16), blocks(q_all[r])).astype(BF16)
        dv = nn(w.T.astype(BF16), datt).astype(BF16)
        dnorm = (
            nt(dq, wq_ref[...]) + nt(dk, wk_ref[...]) + nt(dv, wv_ref[...]) + nt(dpre, wg_ref[...])
        ).astype(BF16).astype(F32)
        dx = standardize_back(dnorm, hat_in[r], sc_in[r][:, 0:1]).astype(BF16).astype(F32)
        total = gm + dx
        for half in range(2):
            t32[pl.ds(2 * r + half, SEQ, stride=8), :] = total[:, half * 128:(half + 1) * 128]
        return carry

    lax.fori_loop(0, 2, backward, 0)

    drain(pr, N_WIDE, recv.at[7])
    zs[...] = jnp.sum(pr[...].astype(F32), axis=0).astype(BF16)
    zr[along] = zs[...]
    push(peer_z, place_z, N_Z, me, zs, zr, send.at[8], recv.at[8], False)

    lax.fori_loop(2, RES, backward, 0)

    os[...] = t32[0:1024, :].reshape(N_DAP, 8, 128).astype(BF16)
    orr[me] = os[me]
    push(peer_all, lambda d: d, N_DAP, me, os, orr, send.at[10], recv.at[10], True)

    drain(zr, N_Z, recv.at[8])
    fs[...] = jnp.sum(zr[...].astype(F32), axis=0).astype(BF16)
    fr[wide] = fs[...]
    push(peer_wide, place_wide, N_WIDE, me, fs, fr, send.at[9], recv.at[9], False)
    drain(xs, N_DAP, send.at[0])
    drain(gs, N_WIDE, send.at[1])
    drain(us, N_DAP, send.at[2])
    drain(rg, N_Z, send.at[3])
    drain(lg, N_WIDE, send.at[4])
    drain(grs, N_Z, send.at[5])
    drain(gls, N_WIDE, send.at[6])
    drain(ps, N_WIDE, send.at[7])
    drain(zr, N_Z, send.at[8])
    drain(fr, N_WIDE, send.at[9])
    drain(fr, N_WIDE, recv.at[9])
    halves = []
    for m in range(16):
        pwg_ref[m * 64:(m + 1) * 64, :] = fr[m, 0:64, :].astype(F32)
        halves.append(fr[m, 64:80, :].astype(F32)[0:8, :])
    owg_t = jnp.concatenate(
        [jnp.concatenate(halves[0:8], axis=0), jnp.concatenate(halves[8:16], axis=0)], axis=1
    )
    owg_ref[...] = owg_t.T

    drain(os, N_DAP, send.at[10])
    drain(orr, N_DAP, recv.at[10])
    t32[0:1024, :] = orr[...].astype(F32).reshape(1024, 128)
    out_ref[:, 0:128] = t32[pl.ds(0, 512, stride=2), :].astype(BF16)
    out_ref[:, 128:256] = t32[pl.ds(1, 512, stride=2), :].astype(BF16)


SCRATCH = (
    [((N_DAP, 8, 128), BF16)] * 4
    + [((16, 128, 128), BF16)] * 2
    + [((2048, 128), F32)]
    + [((RES, SEQ, CH), F32)] * 2
    + [((RES, SEQ, 128), F32)]
    + [((RES, SEQ, CH), F32)] * 2
    + [((RES, SEQ, CH), BF16)] * 3
    + [((RES, HEADS * SEQ, SEQ), F32)]
    + [((RES, SEQ, CH), BF16)]
    + [((RES, SEQ, CH), F32)]
    + [((RES, SEQ, 128), F32)]
    + [((64, CH), BF16)]
    + [((128, 128), BF16), ((16, 128, 128), BF16)]
    + [((128, 128), BF16), ((8, 128, 128), BF16)]
    + [((2048, 128), BF16)]
    + [((32, 128, 256), BF16)]
    + [((512, 256), BF16)]
    + [((32, 32, 2048), BF16)]
    + [((512, 1024), BF16)]
    + [((512, 256), F32)]
    + [((16, 128, 128), BF16)] * 2
    + [((8, 128, 128), BF16)] * 2
    + [((RES, SEQ, 64), BF16)]
    + [((16, 80, 128), BF16)] * 2
    + [((80, 128), BF16), ((8, 80, 128), BF16)]
    + [((80, 128), BF16), ((16, 80, 128), BF16)]
    + [((N_DAP, 8, 128), BF16)] * 2
)


def body(
    aligned_rows,
    asking_projection,
    lookup_projection,
    content_projection,
    sigmoid_projection,
    sigmoid_shift,
    result_projection,
    tensor_mean_projections,
    twofold_projection,
    refreshed_rows_adjoint,
    twofold_change_adjoint,
):
    whole = pl.BlockSpec(memory_space=pltpu.VMEM)
    out, pwg, owg, rfg = pl.pallas_call(
        kernel,
        out_shape=(
            jax.ShapeDtypeStruct((512, CH), BF16),
            jax.ShapeDtypeStruct((1024, 128), F32),
            jax.ShapeDtypeStruct((CH, 64), F32),
            jax.ShapeDtypeStruct((SEQ, 128), F32),
        ),
        in_specs=[whole] * 11,
        out_specs=(whole,) * 4,
        scratch_shapes=[pltpu.VMEM(shape, kind) for shape, kind in SCRATCH]
        + [pltpu.SemaphoreType.DMA((11,)), pltpu.SemaphoreType.DMA((11,))],
        compiler_params=pltpu.CompilerParams(
            collective_id=0, has_side_effects=True, vmem_limit_bytes=56 * 2**20
        ),
        name="evoformer_backward",
    )(
        aligned_rows.reshape(512, CH),
        asking_projection,
        lookup_projection,
        content_projection,
        sigmoid_projection,
        sigmoid_shift.reshape(1, CH),
        result_projection,
        tensor_mean_projections,
        twofold_projection,
        refreshed_rows_adjoint.reshape(512, CH),
        twofold_change_adjoint.reshape(2048, 128),
    )
    return (out.reshape(1, 512, CH), pwg, owg, rfg.reshape(SEQ, RES, 32))


def solution(mesh):
    split = P(("dp", "dap"), None, None)
    in_specs = (split,) + (P(),) * 8 + (split, split)
    out_specs = (split, P("dp", None), P("dp", None), P("dp", "dap", None))
    return jax.shard_map(body, mesh=mesh, in_specs=in_specs, out_specs=out_specs, check_vma=False)
```

```python
import functools

import jax
import jax.numpy as jnp
from jax import lax
from jax.experimental import pallas as pl
from jax.experimental.pallas import tpu as pltpu
from jax.sharding import PartitionSpec as P

HEADS = 8
HEAD_DIM = 32
SEQ = 128
RES = 4
CH = 256
N_DAP = 128
N_WIDE = 16
N_Z = 8
MESH = pl.DeviceIdType.MESH
F32 = jnp.float32
BF16 = jnp.bfloat16


def nn(a, b):
    return lax.dot_general(a, b, (((1,), (0,)), ((), ())), preferred_element_type=F32)


def nt(a, b):
    return lax.dot_general(a, b, (((1,), (1,)), ((), ())), preferred_element_type=F32)


def far_first():
    steps = [
        (dx, dy, dz, dc)
        for dy in range(4) for dz in range(8) for dx in range(2) for dc in range(2)
        if dx or dy or dz or dc
    ]
    return sorted(steps, key=lambda d: -(2 * (d[0] + min(d[1], 4 - d[1]) + min(d[2], 8 - d[2])) + d[3]))


def groups(me):
    x = lax.div(me, 64)
    y = lax.rem(lax.div(me, 16), 4)
    z = lax.rem(lax.div(me, 2), 8)
    core = lax.rem(me, 2)
    step = 1 - 2 * core
    xs = [x * 64, (1 - x) * 64]
    ys = [lax.rem(y + 4 + d * step, 4) * 16 for d in range(4)]
    zs = [lax.rem(z + 8 + d * step, 8) for d in range(8)]
    twice = [place * 2 for place in zs]
    cores = [core, 1 - core]
    everyone = []
    for dx, dy, dz, dc in far_first():
        device = xs[dx] + ys[dy] + twice[dz] + cores[dc]
        everyone.append((device, device))
    wide = []
    for dx, dy, dc in (
        (1, 2, 0), (0, 2, 1), (1, 1, 0), (1, 3, 1), (1, 2, 1), (0, 2, 0), (1, 1, 1), (1, 3, 0),
        (0, 1, 0), (0, 3, 1), (1, 0, 0), (0, 1, 1), (0, 3, 0), (1, 0, 1), (0, 0, 1),
    ):
        line = xs[dx] + ys[dy]
        wide.append((line + z * 2 + cores[dc], lax.div(line, 8) + cores[dc]))
    long = [(xs[0] + ys[0] + twice[dz] + core, zs[dz]) for dz in (4, 3, 5, 2, 6, 1, 7)]
    return (me, everyone), (lax.div(xs[0] + ys[0], 8) + core, wide), (z, long)


def push(group, src, dst, send_sem, recv_sem, spread):
    mine, others = group
    for device, place in others:
        pltpu.make_async_remote_copy(
            src_ref=src.at[place] if spread else src,
            dst_ref=dst.at[mine],
            send_sem=send_sem,
            recv_sem=recv_sem,
            device_id={"dap": device},
            device_id_type=MESH,
        ).start()


def drain(ref, total, sem):
    part = ref.at[pl.ds(0, total - 1)]
    pltpu.make_async_copy(part, part, sem).wait()


def standardize(wide):
    average = jnp.mean(wide, axis=-1, keepdims=True)
    centred = wide - average
    variance = jnp.mean(centred * centred, axis=-1, keepdims=True)
    scale = lax.rsqrt(variance + 1e-05)
    return centred * scale, scale


def standardize_back(grad, hat, scale):
    return scale * (
        grad
        - jnp.mean(grad, axis=-1, keepdims=True)
        - hat * jnp.mean(grad * hat, axis=-1, keepdims=True)
    )


def kernel(
    rows_ref, wq_ref, wk_ref, wv_ref, wg_ref, shift_ref, wo_ref, wf_ref, wp_ref, adj_ref, pair_ref,
    out_ref, pwg_ref, owg_ref, rfg_ref,
    xs, xr, us, ur, gs, gr, t32, u32, hat_in, sc_in, gate, att, q_all, k_all,
    v_all, w_all, nmid, hat_mid, sc_mid, ls, lg, rs, rg, lp, g2, w2, y, xp, pacc, gls, glr, grs, grr,
    dcat, ps, pr, qs, qr, zs, zr, fs, fr, os, orr, send, recv,
):
    me = lax.axis_index("dap")
    whole_group, wide_group, long_group = groups(me)
    wide, along = wide_group[0], long_group[0]
    bar = pltpu.get_barrier_semaphore()
    for device, _ in whole_group[1]:
        pl.semaphore_signal(bar, inc=1, device_id={"dap": device}, device_id_type=MESH)

    def push_all(src, dst, sem):
        push(whole_group, src, dst, send.at[sem], recv.at[sem], True)

    def push_wide(src, dst, sem, spread):
        push(wide_group, src, dst, send.at[sem], recv.at[sem], spread)

    def push_z(src, dst, sem, spread):
        push(long_group, src, dst, send.at[sem], recv.at[sem], spread)

    def stage_rows(ref, dst):
        u32[pl.ds(0, 512, stride=2), :] = ref[:, 0:128].astype(F32)
        u32[pl.ds(1, 512, stride=2), :] = ref[:, 128:256].astype(F32)
        dst[...] = u32[...].reshape(N_DAP, 8, 128).astype(BF16)

    stage_rows(rows_ref, xs)
    xr[me] = xs[me]
    pl.semaphore_wait(bar, N_DAP - 1)

    push_all(xs, xr, 0)

    t32[...] = pair_ref[...].astype(F32)

    def stage_pair(at, carry):
        for core in range(2):
            for i in range(RES):
                parts = [
                    t32[pl.ds(i * 512 + at * 64 + core * 4 + r, 8, stride=8), :] for r in range(RES)
                ]
                gs[at * 2 + core, i * 32:(i + 1) * 32, :] = jnp.concatenate(parts, axis=0).astype(BF16)
        return carry

    lax.fori_loop(0, 8, stage_pair, 0)
    gr[wide] = gs[wide]
    push_wide(gs, gr, 8, True)

    stage_rows(adj_ref, us)
    ur[me] = us[me]
    g2[...] = jnp.zeros_like(g2)
    for c_hi in range(16):
        for c_lo in range(2):
            w2[c_hi * 32:(c_hi + 1) * 32, c_lo * 128:(c_lo + 1) * 128] = (
                wp_ref[(2 * c_hi + c_lo) * 32:(2 * c_hi + c_lo + 1) * 32, :].astype(F32) * (1.0 / SEQ)
            ).astype(BF16)

    drain(xr, N_DAP, recv.at[0])
    u32[...] = xr[...].astype(F32).reshape(1024, 128)

    lane_head = lax.broadcasted_iota(jnp.int32, (1, CH), 1) // HEAD_DIM
    masks = [(lane_head == h).astype(F32).astype(BF16) for h in range(HEADS)]

    def blocks(value):
        return jnp.concatenate([value * m for m in masks], axis=0)

    def side_by_side(value):
        return jnp.concatenate([value[h * 128:(h + 1) * 128, :] for h in range(HEADS)], axis=1)

    def forward(r, carry):
        x = jnp.concatenate(
            [u32[pl.ds(2 * r + half, SEQ, stride=8), :] for half in range(2)], axis=1
        )
        hat, scale = standardize(x)
        hat_in[r] = hat
        sc_in[r] = jnp.broadcast_to(scale, (SEQ, 128))
        normed = hat.astype(BF16)
        q = (nn(normed, wq_ref[...]) * HEAD_DIM ** (-0.5)).astype(BF16)
        k = nn(normed, wk_ref[...]).astype(BF16)
        v = nn(normed, wv_ref[...]).astype(BF16)
        g = jax.nn.sigmoid(nn(normed, wg_ref[...]) + shift_ref[...])
        q_all[r] = q
        k_all[r] = k
        v_all[r] = v
        gate[r] = g
        scores = nt(blocks(q), k)
        e = jnp.exp(scores - jnp.max(scores, axis=-1, keepdims=True))
        w = e * (1.0 / jnp.sum(e, axis=-1, keepdims=True))
        w_all[r] = w
        a = nn(side_by_side(w.astype(BF16)), blocks(v))
        att[r] = a
        gated = (a * g).astype(BF16)
        upd = (x + nn(gated, wo_ref[...])).astype(BF16).astype(F32)
        hat, scale = standardize(upd)
        hat_mid[r] = hat
        sc_mid[r] = jnp.broadcast_to(scale, (SEQ, 128))
        normed = hat.astype(BF16)
        nmid[r] = normed
        factors = nt(wf_ref[...], normed).astype(BF16)
        ls[r] = factors[0:32, :]
        rs[r] = factors[32:64, :]
        push_wide(ls.at[r], lg.at[r], 11 + r, False)
        push_z(rs.at[r], rg.at[r], 15 + r, False)
        lg[r, wide] = ls[r]
        rg[r, along] = rs[r]
        return carry

    lax.fori_loop(0, RES, forward, 0)

    push_all(us, ur, 1)

    drain(gr, N_WIDE, recv.at[8])
    t32[...] = gr[...].astype(F32).reshape(2048, 128)

    def build(jn, carry):
        part = jnp.concatenate(
            [t32[pl.ds(r * 32 + jn, 16, stride=128), :] for r in range(RES)], axis=0
        ).astype(BF16)
        g2[jn, 0:64, 0:128] = part
        g2[jn, 64:128, 128:256] = part
        return carry

    lax.fori_loop(0, 32, build, 0)

    def pair_grad(at, carry):
        res = nt(w2[...], g2[pl.ds(at * 4, 4)].reshape(512, 256)).astype(BF16)
        for jj in range(4):
            for c_hi in range(16):
                y[at * 4 + jj, :, c_hi * 128:(c_hi + 1) * 128] = res[
                    c_hi * 32:(c_hi + 1) * 32, jj * 128:(jj + 1) * 128
                ]
        return carry

    lax.fori_loop(0, 8, pair_grad, 0)

    for r in range(RES):
        drain(lg.at[r], N_WIDE, recv.at[11 + r])
    t32[...] = lg[...].astype(F32).reshape(2048, 128)

    def order_left(c, carry):
        part = jnp.concatenate(
            [t32[pl.ds(r * 512 + c, 16, stride=32), :] for r in range(RES)], axis=0
        )
        lp[pl.ds(pl.multiple_of(c * 64, 64), 64), :] = part.astype(BF16)
        return carry

    lax.fori_loop(0, 32, order_left, 0)

    for r in range(RES):
        drain(rg.at[r], N_Z, recv.at[15 + r])
    rg_t = rg[...].reshape(1024, 128).astype(F32).T.astype(BF16)

    def left_grad(at, carry):
        col = pl.multiple_of(at * 512, 512)
        res = nn(rg_t, y[:, :, pl.ds(col, 512)].reshape(1024, 512))
        t32[0:512, :] = res.T
        for m in range(16):
            gls[at, m] = jnp.concatenate(
                [t32[pl.ds(m + 16 * r, 8, stride=64), :] for r in range(RES)], axis=0
            ).astype(BF16)
        glr[at, wide] = gls[at, wide]
        push_wide(gls.at[at], glr.at[at], 23 + at, True)
        return carry

    lax.fori_loop(0, 4, left_grad, 0)

    def right_grad(r, carry):
        res = nn(y[pl.ds(r * 8, 8)].reshape(256, 2048), lp[...]).astype(BF16)
        grs[r] = res.reshape(8, 32, 128)
        grr[r, along] = grs[r, along]
        push_z(grs.at[r], grr.at[r], 19 + r, True)
        return carry

    lax.fori_loop(0, RES, right_grad, 0)

    pacc[...] = jnp.zeros_like(pacc)

    def pair_weight(r, carry):
        rows = rg[r].reshape(256, 128)
        for group in range(4):
            res = nt(rows, lp[group * 512:(group + 1) * 512, :]).astype(BF16)
            for jj in range(8):
                for cc in range(4):
                    c_hi = group * 4 + cc
                    xp[c_hi * 32:(c_hi + 1) * 32, jj * 128:(jj + 1) * 128] = res[
                        jj * 32:(jj + 1) * 32, cc * 128:(cc + 1) * 128
                    ]
        pacc[...] += nn(xp[...], g2[pl.ds(r * 8, 8)].reshape(1024, 256))
        return carry

    lax.fori_loop(0, RES, pair_weight, 0)

    for m in range(16):
        part = pacc[m * 32:(m + 1) * 32, :] * (1.0 / SEQ)
        ps[m] = jnp.concatenate([part[:, 0:128], part[:, 128:256]], axis=0).astype(BF16)
    pr[wide] = ps[wide]
    push_wide(ps, pr, 27, True)

    for r in range(RES):
        drain(grr.at[r], N_Z, recv.at[19 + r])
    right_sum = jnp.sum(grr[...].astype(F32), axis=1)
    for at in range(4):
        drain(glr.at[at], N_WIDE, recv.at[23 + at])
    left_sum = jnp.sum(glr[...].astype(F32), axis=1)
    owg = jnp.zeros((64, CH), F32)
    for r in range(RES):
        both = jnp.concatenate(
            [left_sum[at, r * 8:(r + 1) * 8, :] for at in range(4)] + [right_sum[r]], axis=0
        )
        owg = owg + nn(both.astype(BF16), nmid[r])
        dcat[r] = both.T.astype(BF16)

    for m in range(16):
        half = m // 8
        qs[m] = jnp.concatenate(
            [
                owg[(m % 8) * 8:(m % 8) * 8 + 8, half * 128:(half + 1) * 128],
                jnp.zeros((8, 128), F32),
            ],
            axis=0,
        ).astype(BF16)
    qr[wide] = qs[wide]
    push_wide(qs, qr, 38, True)

    drain(ur, N_DAP, recv.at[1])
    t32[1024:2048, :] = ur[...].astype(F32).reshape(1024, 128)

    def backward(r, carry):
        grad = nn(dcat[r], wf_ref[...]).astype(BF16).astype(F32)
        dmid = standardize_back(grad, hat_mid[r], sc_mid[r][:, 0:1]).astype(BF16).astype(F32)
        arriving = jnp.concatenate(
            [t32[pl.ds(1024 + 2 * r + half, SEQ, stride=8), :] for half in range(2)], axis=1
        )
        gm16 = (arriving + dmid).astype(BF16)
        gm = gm16.astype(F32)
        dgated = nt(gm16, wo_ref[...]).astype(BF16).astype(F32)
        g = gate[r]
        datt = blocks((dgated * g).astype(BF16))
        dpre = (dgated * att[r] * g * (1.0 - g)).astype(BF16)
        w = w_all[r]
        dw = nt(datt, v_all[r])
        ds = w * (dw - jnp.sum(w * dw, axis=-1, keepdims=True))
        dq = nn(side_by_side(ds.astype(BF16)), blocks(k_all[r])).astype(BF16)
        dq = (dq.astype(F32) * HEAD_DIM ** (-0.5)).astype(BF16)
        dk = nn(ds.T.astype(BF16), blocks(q_all[r])).astype(BF16)
        dv = nn(w.T.astype(BF16), datt).astype(BF16)
        dnorm = (
            nt(dq, wq_ref[...]) + nt(dk, wk_ref[...]) + nt(dv, wv_ref[...]) + nt(dpre, wg_ref[...])
        ).astype(BF16).astype(F32)
        dx = standardize_back(dnorm, hat_in[r], sc_in[r][:, 0:1]).astype(BF16).astype(F32)
        total = gm + dx
        for half in range(2):
            u32[pl.ds(2 * r + half, SEQ, stride=8), :] = total[:, half * 128:(half + 1) * 128]
        return carry

    lax.fori_loop(0, 2, backward, 0)

    drain(pr, N_WIDE, recv.at[27])
    drain(qr, N_WIDE, recv.at[38])
    zs[0:64, :] = jnp.sum(pr[...].astype(F32), axis=0).astype(BF16)
    zs[64:80, :] = jnp.sum(qr[...].astype(F32), axis=0).astype(BF16)
    zr[along] = zs[...]
    push_z(zs, zr, 28, False)

    lax.fori_loop(2, RES, backward, 0)

    os[...] = u32[...].reshape(N_DAP, 8, 128).astype(BF16)
    orr[me] = os[me]
    push_all(os, orr, 2)
    drain(zr, N_Z, recv.at[28])
    fs[...] = jnp.sum(zr[...].astype(F32), axis=0).astype(BF16)
    fr[wide] = fs[...]
    push_wide(fs, fr, 29, False)

    rfg_ref[...] = right_sum.reshape(128, SEQ)
    drain(xr, N_DAP, send.at[0])
    drain(ur, N_DAP, send.at[1])
    for r in range(RES):
        drain(lg.at[r], N_WIDE, send.at[11 + r])
        drain(rg.at[r], N_Z, send.at[15 + r])
        drain(grr.at[r], N_Z, send.at[19 + r])
        drain(glr.at[r], N_WIDE, send.at[23 + r])
    drain(gr, N_WIDE, send.at[8])
    drain(pr, N_WIDE, send.at[27])
    drain(qr, N_WIDE, send.at[38])
    drain(zr, N_Z, send.at[28])

    drain(fr, N_WIDE, recv.at[29])
    halves = []
    for m in range(16):
        pwg_ref[m * 64:(m + 1) * 64, :] = fr[m, 0:64, :].astype(F32)
        halves.append(fr[m, 64:80, :].astype(F32)[0:8, :])
    owg_ref[...] = jnp.concatenate(
        [jnp.concatenate(halves[0:8], axis=0), jnp.concatenate(halves[8:16], axis=0)], axis=1
    )
    drain(fr, N_WIDE, send.at[29])

    drain(orr, N_DAP, recv.at[2])
    u32[...] = orr[...].astype(F32).reshape(1024, 128)
    out_ref[:, 0:128] = u32[pl.ds(0, 512, stride=2), :].astype(BF16)
    out_ref[:, 128:256] = u32[pl.ds(1, 512, stride=2), :].astype(BF16)
    drain(orr, N_DAP, send.at[2])


def settle(*refs):
    found, results, held, arrive, leave = refs[0:4], refs[4:8], refs[8:12], refs[12], refs[13]
    ins = [pltpu.make_async_copy(found[n], held[n], arrive.at[n]) for n in range(4)]
    outs = [pltpu.make_async_copy(held[n], results[n], leave.at[n]) for n in range(4)]
    for copy in ins:
        copy.start()
    for n in range(4):
        ins[n].wait()
        outs[n].start()
    for copy in outs:
        copy.wait()


SCRATCH = (
    [((N_DAP, 8, 128), BF16)] * 4
    + [((16, 128, 128), BF16)] * 2
    + [((2048, 128), F32), ((1024, 128), F32)]
    + [((RES, SEQ, CH), F32)]
    + [((RES, SEQ, 128), F32)]
    + [((RES, SEQ, CH), F32)] * 2
    + [((RES, SEQ, CH), BF16)] * 3
    + [((RES, HEADS * SEQ, SEQ), F32)]
    + [((RES, SEQ, CH), BF16)]
    + [((RES, SEQ, CH), F32)]
    + [((RES, SEQ, 128), F32)]
    + [((RES, 32, 128), BF16), ((RES, 16, 32, 128), BF16)]
    + [((RES, 32, 128), BF16), ((RES, 8, 32, 128), BF16)]
    + [((2048, 128), BF16)]
    + [((32, 128, 256), BF16)]
    + [((512, 256), BF16)]
    + [((32, 32, 2048), BF16)]
    + [((512, 1024), BF16)]
    + [((512, 256), F32)]
    + [((4, 16, 32, 128), BF16)] * 2
    + [((RES, 8, 32, 128), BF16)] * 2
    + [((RES, SEQ, 64), BF16)]
    + [((16, 64, 128), BF16)] * 2
    + [((16, 16, 128), BF16)] * 2
    + [((80, 128), BF16), ((8, 80, 128), BF16)]
    + [((80, 128), BF16), ((16, 80, 128), BF16)]
    + [((N_DAP, 8, 128), BF16)] * 2
)
SEMAPHORES = 39


def body(
    aligned_rows,
    asking_projection,
    lookup_projection,
    content_projection,
    sigmoid_projection,
    sigmoid_shift,
    result_projection,
    tensor_mean_projections,
    twofold_projection,
    refreshed_rows_adjoint,
    twofold_change_adjoint,
):
    whole = pl.BlockSpec(memory_space=pltpu.VMEM)
    results = (
        jax.ShapeDtypeStruct((512, CH), BF16),
        jax.ShapeDtypeStruct((1024, 128), F32),
        jax.ShapeDtypeStruct((64, CH), F32),
        jax.ShapeDtypeStruct((128, SEQ), F32),
    )
    found = pl.pallas_call(
        kernel,
        out_shape=results,
        in_specs=[whole] * 11,
        out_specs=(whole,) * 4,
        scratch_shapes=[pltpu.VMEM(shape, kind) for shape, kind in SCRATCH]
        + [pltpu.SemaphoreType.DMA((SEMAPHORES,)), pltpu.SemaphoreType.DMA((SEMAPHORES,))],
        compiler_params=pltpu.CompilerParams(
            collective_id=0, has_side_effects=True, vmem_limit_bytes=56 * 2**20
        ),
        name="evoformer_backward",
    )(
        aligned_rows.reshape(512, CH),
        asking_projection,
        lookup_projection,
        content_projection,
        sigmoid_projection,
        sigmoid_shift.reshape(1, CH),
        result_projection,
        tensor_mean_projections.T,
        twofold_projection,
        refreshed_rows_adjoint.reshape(512, CH),
        twofold_change_adjoint.reshape(2048, 128),
    )
    anywhere = pl.BlockSpec(memory_space=pl.ANY)
    out, pwg, owg, rfg = pl.pallas_call(
        settle,
        out_shape=results,
        in_specs=[anywhere] * 4,
        out_specs=(anywhere,) * 4,
        scratch_shapes=[pltpu.VMEM(result.shape, result.dtype) for result in results]
        + [pltpu.SemaphoreType.DMA((4,)), pltpu.SemaphoreType.DMA((4,))],
        name="settle",
    )(*found)
    return (
        out.reshape(1, 512, CH),
        pwg,
        owg.T,
        rfg.reshape(RES, 32, SEQ).transpose(2, 0, 1),
    )


def solution(mesh):
    split = P(("dp", "dap"), None, None)
    in_specs = (split,) + (P(),) * 8 + (split, split)
    out_specs = (split, P("dp", None), P("dp", None), P("dp", "dap", None))
    return jax.shard_map(body, mesh=mesh, in_specs=in_specs, out_specs=out_specs, check_vma=False)
```

```python
import functools

import jax
import jax.numpy as jnp
from jax import lax
from jax.experimental import pallas as pl
from jax.experimental.pallas import tpu as pltpu
from jax.sharding import PartitionSpec as P

HEADS = 8
HEAD_DIM = 32
SEQ = 128
RES = 4
CH = 256
N_DAP = 128
N_WIDE = 16
N_Z = 8
MESH = pl.DeviceIdType.MESH
F32 = jnp.float32
BF16 = jnp.bfloat16


def nn(a, b):
    return lax.dot_general(a, b, (((1,), (0,)), ((), ())), preferred_element_type=F32)


def nt(a, b):
    return lax.dot_general(a, b, (((1,), (1,)), ((), ())), preferred_element_type=F32)


def far_first():
    steps = [
        (dx, dy, dz, dc)
        for dy in range(4) for dz in range(8) for dx in range(2) for dc in range(2)
        if dx or dy or dz or dc
    ]
    return sorted(steps, key=lambda d: -(2 * (d[0] + min(d[1], 4 - d[1]) + min(d[2], 8 - d[2])) + d[3]))


def groups(me):
    x = lax.div(me, 64)
    y = lax.rem(lax.div(me, 16), 4)
    z = lax.rem(lax.div(me, 2), 8)
    core = lax.rem(me, 2)
    step = 1 - 2 * core
    xs = [x * 64, (1 - x) * 64]
    ys = [lax.rem(y + 4 + d * step, 4) * 16 for d in range(4)]
    zs = [lax.rem(z + 8 + d * step, 8) for d in range(8)]
    twice = [place * 2 for place in zs]
    cores = [core, 1 - core]
    everyone = []
    for dx, dy, dz, dc in far_first():
        device = xs[dx] + ys[dy] + twice[dz] + cores[dc]
        everyone.append((device, device))
    wide = []
    for dx, dy, dc in (
        (1, 2, 0), (0, 2, 1), (1, 1, 0), (1, 3, 1), (1, 2, 1), (0, 2, 0), (1, 1, 1), (1, 3, 0),
        (0, 1, 0), (0, 3, 1), (1, 0, 0), (0, 1, 1), (0, 3, 0), (1, 0, 1), (0, 0, 1),
    ):
        line = xs[dx] + ys[dy]
        wide.append((line + z * 2 + cores[dc], lax.div(line, 8) + cores[dc]))
    long = [(xs[0] + ys[0] + twice[dz] + core, zs[dz]) for dz in (4, 3, 5, 2, 6, 1, 7)]
    return (me, everyone), (lax.div(xs[0] + ys[0], 8) + core, wide), (z, long)


def push(group, src, dst, send_sem, recv_sem, spread):
    mine, others = group
    for device, place in others:
        pltpu.make_async_remote_copy(
            src_ref=src.at[place] if spread else src,
            dst_ref=dst.at[mine],
            send_sem=send_sem,
            recv_sem=recv_sem,
            device_id={"dap": device},
            device_id_type=MESH,
        ).start()


def drain(ref, total, sem):
    part = ref.at[pl.ds(0, total - 1)]
    pltpu.make_async_copy(part, part, sem).wait()


def standardize(wide):
    average = jnp.mean(wide, axis=-1, keepdims=True)
    centred = wide - average
    variance = jnp.mean(centred * centred, axis=-1, keepdims=True)
    scale = lax.rsqrt(variance + 1e-05)
    return centred * scale, scale


def standardize_back(grad, hat, scale):
    return scale * (
        grad
        - jnp.mean(grad, axis=-1, keepdims=True)
        - hat * jnp.mean(grad * hat, axis=-1, keepdims=True)
    )


def kernel(
    rows_in, wq_in, wk_in, wv_in, wg_in, shift_in, wo_in, wf_in, wp_in, adj_in, pair_in,
    out_ref, pwg_ref, owg_ref, rfg_ref,
    rows_ref, wq_ref, wk_ref, wv_ref, wg_ref, shift_ref, wo_ref, wf_ref, wp_ref, adj_ref, pair_ref,
    xs, xr, us, ur, gs, gr, t32, u32, hat_in, sc_in, gate, att, q_all, k_all,
    v_all, w_all, nmid, hat_mid, sc_mid, ls, lg, rs, rg, lp, g2, w2, y, xp, pacc, gls, glr, grs, grr,
    dcat, ps, pr, qs, qr, zs, zr, fs, fr, os, orr, w_t, send, recv, bring,
):
    me = lax.axis_index("dap")
    whole_group, wide_group, long_group = groups(me)
    wide, along = wide_group[0], long_group[0]
    pairs = (
        (rows_in, rows_ref), (pair_in, pair_ref), (adj_in, adj_ref), (wp_in, wp_ref), (wq_in, wq_ref),
        (wk_in, wk_ref), (wv_in, wv_ref), (wg_in, wg_ref), (shift_in, shift_ref), (wo_in, wo_ref),
        (wf_in, wf_ref),
    )
    brought = [pltpu.make_async_copy(a, b, bring.at[n]) for n, (a, b) in enumerate(pairs)]
    for copy in brought:
        copy.start()
    bar = pltpu.get_barrier_semaphore()
    for device, _ in whole_group[1]:
        pl.semaphore_signal(bar, inc=1, device_id={"dap": device}, device_id_type=MESH)

    def push_all(src, dst, sem):
        push(whole_group, src, dst, send.at[sem], recv.at[sem], True)

    def push_wide(src, dst, sem, spread):
        push(wide_group, src, dst, send.at[sem], recv.at[sem], spread)

    def push_z(src, dst, sem, spread):
        push(long_group, src, dst, send.at[sem], recv.at[sem], spread)

    def stage_rows(ref):
        u32[pl.ds(0, 512, stride=2), :] = ref[:, 0:128].astype(F32)
        u32[pl.ds(1, 512, stride=2), :] = ref[:, 128:256].astype(F32)

    brought[0].wait()
    stage_rows(rows_ref)
    for p in range(2):
        xs[p] = u32[...].reshape(N_DAP, 8, 128)[:, 4 * p:4 * p + 4, :].astype(BF16)
        xr[p, me] = xs[p, me]
    pl.semaphore_wait(bar, N_DAP - 1)

    for p in range(2):
        push_all(xs.at[p], xr.at[p], p)

    brought[1].wait()
    t32[...] = pair_ref[...].astype(F32)

    def stage_pair(at, carry):
        for core in range(2):
            for i in range(RES):
                parts = [
                    t32[pl.ds(i * 512 + at * 64 + core * 4 + r, 8, stride=8), :] for r in range(RES)
                ]
                gs[at * 2 + core, i * 32:(i + 1) * 32, :] = jnp.concatenate(parts, axis=0).astype(BF16)
        return carry

    lax.fori_loop(0, 8, stage_pair, 0)
    gr[wide] = gs[wide]
    push_wide(gs, gr, 8, True)

    for copy in brought[2:]:
        copy.wait()
    stage_rows(adj_ref)
    us[...] = u32[...].reshape(N_DAP, 8, 128).astype(BF16)
    ur[me] = us[me]
    g2[...] = jnp.zeros_like(g2)
    for c_hi in range(16):
        for c_lo in range(2):
            w2[c_hi * 32:(c_hi + 1) * 32, c_lo * 128:(c_lo + 1) * 128] = (
                wp_ref[(2 * c_hi + c_lo) * 32:(2 * c_hi + c_lo + 1) * 32, :].astype(F32) * (1.0 / SEQ)
            ).astype(BF16)

    lane_head = lax.broadcasted_iota(jnp.int32, (1, CH), 1) // HEAD_DIM
    masks = [(lane_head == h).astype(F32).astype(BF16) for h in range(HEADS)]

    def blocks(value):
        return jnp.concatenate([value * m for m in masks], axis=0)

    def side_by_side(value):
        return jnp.concatenate([value[h * 128:(h + 1) * 128, :] for h in range(HEADS)], axis=1)

    def forward(r, n):
        x = jnp.concatenate(
            [u32[pl.ds(2 * n + half, SEQ, stride=4), :] for half in range(2)], axis=1
        )
        hat, scale = standardize(x)
        hat_in[r] = hat
        sc_in[r] = jnp.broadcast_to(scale, (SEQ, 128))
        normed = hat.astype(BF16)
        q = (nn(normed, wq_ref[...]) * HEAD_DIM ** (-0.5)).astype(BF16)
        k = nn(normed, wk_ref[...]).astype(BF16)
        v = nn(normed, wv_ref[...]).astype(BF16)
        g = jax.nn.sigmoid(nn(normed, wg_ref[...]) + shift_ref[...])
        q_all[r] = q
        k_all[r] = k
        v_all[r] = v
        gate[r] = g
        scores = nt(blocks(q), k)
        e = jnp.exp(scores - jnp.max(scores, axis=-1, keepdims=True))
        w = e * (1.0 / jnp.sum(e, axis=-1, keepdims=True))
        w_all[r] = w
        a = nn(side_by_side(w.astype(BF16)), blocks(v))
        att[r] = a
        gated = (a * g).astype(BF16)
        upd = (x + nn(gated, wo_ref[...])).astype(BF16).astype(F32)
        hat, scale = standardize(upd)
        hat_mid[r] = hat
        sc_mid[r] = jnp.broadcast_to(scale, (SEQ, 128))
        normed = hat.astype(BF16)
        nmid[r] = normed
        factors = nt(wf_ref[...], normed).astype(BF16)
        return factors

    def forward_pair(p, carry):
        drain(xr.at[p], N_DAP, recv.at[p])
        u32[0:512, :] = xr[p].astype(F32).reshape(512, 128)
        both = [forward(2 * p + n, n) for n in range(2)]
        ls[p] = jnp.concatenate([factors[0:32, :] for factors in both], axis=0)
        rs[p] = jnp.concatenate([factors[32:64, :] for factors in both], axis=0)
        push_z(rs.at[p], rg.at[p], 15 + p, False)
        push_wide(ls.at[p], lg.at[p], 11 + p, False)
        lg[p, wide] = ls[p]
        rg[p, along] = rs[p]
        return carry

    lax.fori_loop(0, 2, forward_pair, 0)

    push_all(us, ur, 2)

    drain(gr, N_WIDE, recv.at[8])
    t32[...] = gr[...].astype(F32).reshape(2048, 128)

    for jn in range(32):
        from_j = (jn // 16 * 2 + jn % 2) * 8 + jn % 16 // 2
        part = jnp.concatenate(
            [t32[pl.ds(r * 32 + from_j, 16, stride=128), :] for r in range(RES)], axis=0
        ).astype(BF16)
        g2[jn, 0:64, 0:128] = part
        g2[jn, 64:128, 128:256] = part

    for at in range(8):
        res = nt(w2[...], g2[at * 4:at * 4 + 4].reshape(512, 256)).astype(BF16)
        for jj in range(4):
            for c_hi in range(16):
                y[at * 4 + jj, :, c_hi * 128:(c_hi + 1) * 128] = res[
                    c_hi * 32:(c_hi + 1) * 32, jj * 128:(jj + 1) * 128
                ]
    for r in range(RES):
        w_t[r] = w_all[r].astype(BF16).T

    for p in range(2):
        drain(lg.at[p], N_WIDE, recv.at[11 + p])
    t32[...] = lg[...].astype(F32).reshape(2048, 128)
    for c in range(32):
        part = jnp.concatenate(
            [
                t32[pl.ds((r // 2) * 1024 + (r % 2) * 32 + c, 16, stride=64), :]
                for r in range(RES)
            ],
            axis=0,
        )
        lp[c * 64:(c + 1) * 64, :] = part.astype(BF16)

    for p in range(2):
        res = nn(y[p * 16:(p + 1) * 16].reshape(512, 2048), lp[...]).astype(BF16)
        grs[p] = res.reshape(8, 64, 128)
    for p in range(2):
        grr[p, along] = grs[p, along]
        push_z(grs.at[p], grr.at[p], 19 + p, True)

    for p in range(2):
        drain(rg.at[p], N_Z, recv.at[15 + p])
    rg_t = rg[...].reshape(1024, 128).astype(F32).T.astype(BF16)
    for at in range(4):
        res = nn(rg_t, y[:, :, at * 512:(at + 1) * 512].reshape(1024, 512))
        t32[at * 512:(at + 1) * 512, :] = res.T
    for m in range(16):
        gls[m] = jnp.concatenate(
            [t32[pl.ds(m + 16 * r, 32, stride=64), :] for r in range(RES)], axis=0
        ).astype(BF16)
    glr[wide] = gls[wide]
    push_wide(gls, glr, 23, True)

    for group in range(4):
        res = nt(rg[...].reshape(1024, 128), lp[group * 512:(group + 1) * 512, :]).astype(BF16)
        for jn in range(32):
            for cc in range(4):
                c_hi = group * 4 + cc
                xp[c_hi * 32:(c_hi + 1) * 32, jn * 128:(jn + 1) * 128] = res[
                    jn * 32:(jn + 1) * 32, cc * 128:(cc + 1) * 128
                ]
    pacc[...] = nn(xp[...], g2[...].reshape(4096, 256))

    for m in range(16):
        part = pacc[m * 32:(m + 1) * 32, :] * (1.0 / SEQ)
        ps[m] = jnp.concatenate([part[:, 0:128], part[:, 128:256]], axis=0).astype(BF16)
    pr[wide] = ps[wide]
    push_wide(ps, pr, 27, True)

    for p in range(2):
        drain(grr.at[p], N_Z, recv.at[19 + p])
    right_sum = jnp.sum(grr[...].astype(F32), axis=1).reshape(128, SEQ)
    drain(glr, N_WIDE, recv.at[23])
    left_sum = jnp.sum(glr[...].astype(F32), axis=0)
    owg = jnp.zeros((64, CH), F32)
    for r in range(RES):
        both = jnp.concatenate(
            [left_sum[r * 32:(r + 1) * 32, :], right_sum[r * 32:(r + 1) * 32, :]], axis=0
        )
        owg = owg + nn(both.astype(BF16), nmid[r])
        dcat[r] = both.T.astype(BF16)

    for m in range(16):
        half = m // 8
        qs[m] = jnp.concatenate(
            [
                owg[(m % 8) * 8:(m % 8) * 8 + 8, half * 128:(half + 1) * 128],
                jnp.zeros((8, 128), F32),
            ],
            axis=0,
        ).astype(BF16)
    qr[wide] = qs[wide]
    push_wide(qs, qr, 38, True)

    drain(ur, N_DAP, recv.at[2])
    t32[1024:2048, :] = ur[...].astype(F32).reshape(1024, 128)

    def backward(r, n):
        grad = nn(dcat[r], wf_ref[...]).astype(BF16).astype(F32)
        dmid = standardize_back(grad, hat_mid[r], sc_mid[r][:, 0:1]).astype(BF16).astype(F32)
        arriving = jnp.concatenate(
            [t32[pl.ds(1024 + 2 * r + half, SEQ, stride=8), :] for half in range(2)], axis=1
        )
        gm16 = (arriving + dmid).astype(BF16)
        gm = gm16.astype(F32)
        dgated = nt(gm16, wo_ref[...]).astype(BF16).astype(F32)
        g = gate[r]
        datt = blocks((dgated * g).astype(BF16))
        dpre = (dgated * att[r] * g * (1.0 - g)).astype(BF16)
        w = w_all[r]
        dw = nt(datt, v_all[r])
        ds = w * (dw - jnp.sum(w * dw, axis=-1, keepdims=True))
        dq = nn(side_by_side(ds.astype(BF16)), blocks(k_all[r])).astype(BF16)
        dq = (dq.astype(F32) * HEAD_DIM ** (-0.5)).astype(BF16)
        dk = nn(ds.T.astype(BF16), blocks(q_all[r])).astype(BF16)
        dv = nn(w_t[r], datt).astype(BF16)
        dnorm = (
            nt(dq, wq_ref[...]) + nt(dk, wk_ref[...]) + nt(dv, wv_ref[...]) + nt(dpre, wg_ref[...])
        ).astype(BF16).astype(F32)
        dx = standardize_back(dnorm, hat_in[r], sc_in[r][:, 0:1]).astype(BF16).astype(F32)
        total = gm + dx
        for half in range(2):
            u32[pl.ds(2 * n + half, SEQ, stride=4), :] = total[:, half * 128:(half + 1) * 128]

    def backward_pair(p):
        for n in range(2):
            backward(2 * p + n, n)
        os[p] = u32[0:512, :].reshape(N_DAP, 4, 128).astype(BF16)
        orr[p, me] = os[p, me]
        push_all(os.at[p], orr.at[p], 3 + p)

    backward_pair(0)

    drain(pr, N_WIDE, recv.at[27])
    drain(qr, N_WIDE, recv.at[38])
    zs[0:64, :] = jnp.sum(pr[...].astype(F32), axis=0).astype(BF16)
    zs[64:80, :] = jnp.sum(qr[...].astype(F32), axis=0).astype(BF16)
    zr[along] = zs[...]
    push_z(zs, zr, 28, False)

    backward_pair(1)

    drain(zr, N_Z, recv.at[28])
    fs[...] = jnp.sum(zr[...].astype(F32), axis=0).astype(BF16)
    fr[wide] = fs[...]
    push_wide(fs, fr, 29, False)

    rfg_ref[...] = right_sum
    drain(xr.at[0], N_DAP, send.at[0])
    drain(xr.at[1], N_DAP, send.at[1])
    drain(ur, N_DAP, send.at[2])
    for p in range(2):
        drain(lg.at[p], N_WIDE, send.at[11 + p])
        drain(rg.at[p], N_Z, send.at[15 + p])
        drain(grr.at[p], N_Z, send.at[19 + p])
    drain(glr, N_WIDE, send.at[23])
    drain(gr, N_WIDE, send.at[8])
    drain(pr, N_WIDE, send.at[27])
    drain(qr, N_WIDE, send.at[38])
    drain(zr, N_Z, send.at[28])

    drain(fr, N_WIDE, recv.at[29])
    halves = []
    for m in range(16):
        pwg_ref[m * 64:(m + 1) * 64, :] = fr[m, 0:64, :].astype(F32)
        halves.append(fr[m, 64:80, :].astype(F32)[0:8, :])
    owg_ref[...] = jnp.concatenate(
        [jnp.concatenate(halves[0:8], axis=0), jnp.concatenate(halves[8:16], axis=0)], axis=1
    )
    drain(fr, N_WIDE, send.at[29])

    for p in range(2):
        drain(orr.at[p], N_DAP, recv.at[3 + p])
        t32[0:512, :] = orr[p].astype(F32).reshape(512, 128)
        for k in range(4):
            u32[pl.ds(4 * p + k, N_DAP, stride=8), :] = t32[pl.ds(k, N_DAP, stride=4), :]
    out_ref[:, 0:128] = u32[pl.ds(0, 512, stride=2), :].astype(BF16)
    out_ref[:, 128:256] = u32[pl.ds(1, 512, stride=2), :].astype(BF16)
    drain(orr.at[0], N_DAP, send.at[3])
    drain(orr.at[1], N_DAP, send.at[4])


def settle(*refs):
    found, results, sems = refs[0:4], refs[4:8], refs[8]
    copies = [pltpu.make_async_copy(found[n], results[n], sems.at[n]) for n in range(4)]
    for copy in copies:
        copy.start()
    for copy in copies:
        copy.wait()


SCRATCH = (
    [((512, CH), BF16)]
    + [((CH, CH), BF16)] * 4
    + [((1, CH), F32), ((CH, CH), BF16), ((64, CH), BF16), ((1024, 128), BF16)]
    + [((512, CH), BF16), ((2048, 128), BF16)]
    + [((2, N_DAP, 4, 128), BF16)] * 2
    + [((N_DAP, 8, 128), BF16)] * 2
    + [((16, 128, 128), BF16)] * 2
    + [((2048, 128), F32), ((1024, 128), F32)]
    + [((RES, SEQ, CH), F32)]
    + [((RES, SEQ, 128), F32)]
    + [((RES, SEQ, CH), F32)] * 2
    + [((RES, SEQ, CH), BF16)] * 3
    + [((RES, HEADS * SEQ, SEQ), F32)]
    + [((RES, SEQ, CH), BF16)]
    + [((RES, SEQ, CH), F32)]
    + [((RES, SEQ, 128), F32)]
    + [((2, 64, 128), BF16), ((2, 16, 64, 128), BF16)]
    + [((2, 64, 128), BF16), ((2, 8, 64, 128), BF16)]
    + [((2048, 128), BF16)]
    + [((32, 128, 256), BF16)]
    + [((512, 256), BF16)]
    + [((32, 32, 2048), BF16)]
    + [((512, 4096), BF16)]
    + [((512, 256), F32)]
    + [((16, 128, 128), BF16)] * 2
    + [((2, 8, 64, 128), BF16)] * 2
    + [((RES, SEQ, 64), BF16)]
    + [((16, 64, 128), BF16)] * 2
    + [((16, 16, 128), BF16)] * 2
    + [((80, 128), BF16), ((8, 80, 128), BF16)]
    + [((80, 128), BF16), ((16, 80, 128), BF16)]
    + [((2, N_DAP, 4, 128), BF16)] * 2
    + [((RES, SEQ, HEADS * SEQ), BF16)]
)
SEMAPHORES = 39


def body(
    aligned_rows,
    asking_projection,
    lookup_projection,
    content_projection,
    sigmoid_projection,
    sigmoid_shift,
    result_projection,
    tensor_mean_projections,
    twofold_projection,
    refreshed_rows_adjoint,
    twofold_change_adjoint,
):
    whole = pl.BlockSpec(memory_space=pltpu.VMEM)
    anywhere = pl.BlockSpec(memory_space=pl.ANY)
    results = (
        jax.ShapeDtypeStruct((512, CH), BF16),
        jax.ShapeDtypeStruct((1024, 128), F32),
        jax.ShapeDtypeStruct((64, CH), F32),
        jax.ShapeDtypeStruct((128, SEQ), F32),
    )
    found = pl.pallas_call(
        kernel,
        out_shape=tuple(pltpu.VMEM(result.shape, result.dtype) for result in results),
        in_specs=[anywhere] * 11,
        out_specs=(whole,) * 4,
        scratch_shapes=[pltpu.VMEM(shape, kind) for shape, kind in SCRATCH]
        + [pltpu.SemaphoreType.DMA((SEMAPHORES,)), pltpu.SemaphoreType.DMA((SEMAPHORES,))]
        + [pltpu.SemaphoreType.DMA((11,))],
        compiler_params=pltpu.CompilerParams(
            collective_id=0, has_side_effects=True, vmem_limit_bytes=56 * 2**20
        ),
        name="evoformer_backward",
    )(
        aligned_rows.reshape(512, CH),
        asking_projection,
        lookup_projection,
        content_projection,
        sigmoid_projection,
        sigmoid_shift.reshape(1, CH),
        result_projection,
        tensor_mean_projections.T,
        twofold_projection,
        refreshed_rows_adjoint.reshape(512, CH),
        twofold_change_adjoint.reshape(2048, 128),
    )
    out, pwg, owg, rfg = pl.pallas_call(
        settle,
        out_shape=results,
        in_specs=[anywhere] * 4,
        out_specs=(anywhere,) * 4,
        scratch_shapes=[pltpu.SemaphoreType.DMA((4,))],
        name="settle",
    )(*[pltpu.with_memory_space_constraint(array, pltpu.VMEM) for array in found])
    return (
        out.reshape(1, 512, CH),
        pwg,
        owg.T,
        rfg.reshape(RES, 32, SEQ).transpose(2, 0, 1),
    )


def solution(mesh):
    split = P(("dp", "dap"), None, None)
    in_specs = (split,) + (P(),) * 8 + (split, split)
    out_specs = (split, P("dp", None), P("dp", None), P("dp", "dap", None))
    return jax.shard_map(body, mesh=mesh, in_specs=in_specs, out_specs=out_specs, check_vma=False)
```

```python
import functools

import jax
import jax.numpy as jnp
from jax import lax
from jax.experimental import pallas as pl
from jax.experimental.pallas import tpu as pltpu
from jax.sharding import PartitionSpec as P

HEADS = 8
HEAD_DIM = 32
SEQ = 128
RES = 4
CH = 256
N_DAP = 128
N_WIDE = 16
N_Z = 8
MESH = pl.DeviceIdType.MESH
F32 = jnp.float32
BF16 = jnp.bfloat16


def nn(a, b):
    return lax.dot_general(a, b, (((1,), (0,)), ((), ())), preferred_element_type=F32)


def nt(a, b):
    return lax.dot_general(a, b, (((1,), (1,)), ((), ())), preferred_element_type=F32)


def far_first():
    steps = [
        (dx, dy, dz, dc)
        for dy in range(4) for dz in range(8) for dx in range(2) for dc in range(2)
        if dx or dy or dz or dc
    ]
    return sorted(steps, key=lambda d: -(2 * (d[0] + min(d[1], 4 - d[1]) + min(d[2], 8 - d[2])) + d[3]))


def groups(me):
    x = lax.div(me, 64)
    y = lax.rem(lax.div(me, 16), 4)
    z = lax.rem(lax.div(me, 2), 8)
    core = lax.rem(me, 2)
    step = 1 - 2 * core
    xs = [x * 64, (1 - x) * 64]
    ys = [lax.rem(y + 4 + d * step, 4) * 16 for d in range(4)]
    zs = [lax.rem(z + 8 + d * step, 8) for d in range(8)]
    twice = [place * 2 for place in zs]
    cores = [core, 1 - core]
    everyone = []
    for dx, dy, dz, dc in far_first():
        device = xs[dx] + ys[dy] + twice[dz] + cores[dc]
        everyone.append((device, device))
    wide = []
    for dx, dy, dc in (
        (1, 2, 0), (0, 2, 1), (1, 1, 0), (1, 3, 1), (1, 2, 1), (0, 2, 0), (1, 1, 1), (1, 3, 0),
        (0, 1, 0), (0, 3, 1), (1, 0, 0), (0, 1, 1), (0, 3, 0), (1, 0, 1), (0, 0, 1),
    ):
        line = xs[dx] + ys[dy]
        wide.append((line + z * 2 + cores[dc], lax.div(line, 8) + cores[dc]))
    long = [(xs[0] + ys[0] + twice[dz] + core, zs[dz]) for dz in (4, 3, 5, 2, 6, 1, 7)]
    level = []
    for dx, dy in ((1, 2), (0, 2), (1, 1), (1, 3), (0, 1), (0, 3), (1, 0)):
        line = xs[dx] + ys[dy]
        level.append((line + z * 2 + core, lax.div(line, 16)))
    line = xs[0] + ys[0]
    return (
        (me, everyone),
        (lax.div(line, 8) + core, wide),
        (z, long),
        (lax.div(line, 16), level),
        line + z * 2 + 1 - core,
    )


def push(group, src, dst, send_sem, recv_sem, spread):
    mine, others = group
    for device, place in others:
        pltpu.make_async_remote_copy(
            src_ref=src.at[place] if spread else src,
            dst_ref=dst.at[mine],
            send_sem=send_sem,
            recv_sem=recv_sem,
            device_id={"dap": device},
            device_id_type=MESH,
        ).start()


def drain(ref, total, sem):
    part = ref.at[pl.ds(0, total - 1)]
    pltpu.make_async_copy(part, part, sem).wait()


def standardize(wide):
    average = jnp.mean(wide, axis=-1, keepdims=True)
    centred = wide - average
    variance = jnp.mean(centred * centred, axis=-1, keepdims=True)
    scale = lax.rsqrt(variance + 1e-05)
    return centred * scale, scale


def standardize_back(grad, hat, scale):
    return scale * (
        grad
        - jnp.mean(grad, axis=-1, keepdims=True)
        - hat * jnp.mean(grad * hat, axis=-1, keepdims=True)
    )


def kernel(
    rows_in, wq_in, wk_in, wv_in, wg_in, shift_in, wo_in, wf_in, wp_in, adj_in, pair_in,
    out_ref, pwg_ref, owg_ref, rfg_ref,
    rows_ref, wq_ref, wk_ref, wv_ref, wg_ref, shift_ref, wo_ref, wf_ref, wp_ref, adj_ref, pair_ref,
    xs, xr, us, ur, gs, gr, t32, u32, hat_in, sc_in, gate, att, q_all, k_all,
    v_all, w_all, nmid, hat_mid, sc_mid, ls, lg, rs, rg, lp, g2, w2, y, xp, pacc, gls, glx, glo, glr, grs, grr,
    dcat, ps, pr, qs, qr, zs, zr, zq, zqr, fs, fr, fq, fqr, os, orr, w_t, send, recv, bring,
):
    me = lax.axis_index("dap")
    whole_group, wide_group, long_group, level_group, sibling = groups(me)
    wide, along, level = wide_group[0], long_group[0], level_group[0]
    core_here = lax.rem(me, 2)
    pairs = (
        (rows_in, rows_ref), (pair_in, pair_ref), (adj_in, adj_ref), (wp_in, wp_ref), (wq_in, wq_ref),
        (wk_in, wk_ref), (wv_in, wv_ref), (wg_in, wg_ref), (shift_in, shift_ref), (wo_in, wo_ref),
        (wf_in, wf_ref),
    )
    brought = [pltpu.make_async_copy(a, b, bring.at[n]) for n, (a, b) in enumerate(pairs)]
    for copy in brought:
        copy.start()
    bar = pltpu.get_barrier_semaphore()
    for device, _ in whole_group[1]:
        pl.semaphore_signal(bar, inc=1, device_id={"dap": device}, device_id_type=MESH)

    def push_all(src, dst, sem):
        push(whole_group, src, dst, send.at[sem], recv.at[sem], True)

    def push_wide(src, dst, sem, spread):
        push(wide_group, src, dst, send.at[sem], recv.at[sem], spread)

    def push_z(src, dst, sem, spread):
        push(long_group, src, dst, send.at[sem], recv.at[sem], spread)

    def stage_rows(ref):
        u32[pl.ds(0, 512, stride=2), :] = ref[:, 0:128].astype(F32)
        u32[pl.ds(1, 512, stride=2), :] = ref[:, 128:256].astype(F32)

    brought[0].wait()
    stage_rows(rows_ref)
    for p in range(2):
        xs[p] = u32[...].reshape(N_DAP, 8, 128)[:, 4 * p:4 * p + 4, :].astype(BF16)
        xr[p, me] = xs[p, me]
    pl.semaphore_wait(bar, N_DAP - 1)

    for p in range(2):
        push_all(xs.at[p], xr.at[p], p)

    brought[1].wait()
    t32[...] = pair_ref[...].astype(F32)

    def stage_pair(at, carry):
        for core in range(2):
            for i in range(RES):
                parts = [
                    t32[pl.ds(i * 512 + at * 64 + core * 4 + r, 8, stride=8), :] for r in range(RES)
                ]
                gs[at * 2 + core, i * 32:(i + 1) * 32, :] = jnp.concatenate(parts, axis=0).astype(BF16)
        return carry

    lax.fori_loop(0, 8, stage_pair, 0)
    gr[wide] = gs[wide]
    push_wide(gs, gr, 8, True)

    for copy in brought[2:]:
        copy.wait()
    stage_rows(adj_ref)
    us[...] = u32[...].reshape(N_DAP, 8, 128).astype(BF16)
    ur[me] = us[me]
    g2[...] = jnp.zeros_like(g2)
    for c_hi in range(16):
        for c_lo in range(2):
            w2[c_hi * 32:(c_hi + 1) * 32, c_lo * 128:(c_lo + 1) * 128] = (
                wp_ref[(2 * c_hi + c_lo) * 32:(2 * c_hi + c_lo + 1) * 32, :].astype(F32) * (1.0 / SEQ)
            ).astype(BF16)

    lane_head = lax.broadcasted_iota(jnp.int32, (1, CH), 1) // HEAD_DIM
    masks = [(lane_head == h).astype(F32).astype(BF16) for h in range(HEADS)]

    def blocks(value):
        return jnp.concatenate([value * m for m in masks], axis=0)

    def side_by_side(value):
        return jnp.concatenate([value[h * 128:(h + 1) * 128, :] for h in range(HEADS)], axis=1)

    def forward(r, n):
        x = jnp.concatenate(
            [u32[pl.ds(2 * n + half, SEQ, stride=4), :] for half in range(2)], axis=1
        )
        hat, scale = standardize(x)
        hat_in[r] = hat
        sc_in[r] = jnp.broadcast_to(scale, (SEQ, 128))
        normed = hat.astype(BF16)
        q = (nn(normed, wq_ref[...]) * HEAD_DIM ** (-0.5)).astype(BF16)
        k = nn(normed, wk_ref[...]).astype(BF16)
        v = nn(normed, wv_ref[...]).astype(BF16)
        g = jax.nn.sigmoid(nn(normed, wg_ref[...]) + shift_ref[...])
        q_all[r] = q
        k_all[r] = k
        v_all[r] = v
        gate[r] = g
        scores = nt(blocks(q), k)
        e = jnp.exp(scores - jnp.max(scores, axis=-1, keepdims=True))
        w = e * (1.0 / jnp.sum(e, axis=-1, keepdims=True))
        w_all[r] = w
        a = nn(side_by_side(w.astype(BF16)), blocks(v))
        att[r] = a
        gated = (a * g).astype(BF16)
        upd = (x + nn(gated, wo_ref[...])).astype(BF16).astype(F32)
        hat, scale = standardize(upd)
        hat_mid[r] = hat
        sc_mid[r] = jnp.broadcast_to(scale, (SEQ, 128))
        normed = hat.astype(BF16)
        nmid[r] = normed
        factors = nt(wf_ref[...], normed).astype(BF16)
        return factors

    def forward_pair(p, carry):
        drain(xr.at[p], N_DAP, recv.at[p])
        u32[0:512, :] = xr[p].astype(F32).reshape(512, 128)
        both = [forward(2 * p + n, n) for n in range(2)]
        ls[p] = jnp.concatenate([factors[0:32, :] for factors in both], axis=0)
        rs[p] = jnp.concatenate([factors[32:64, :] for factors in both], axis=0)
        push_z(rs.at[p], rg.at[p], 15 + p, False)
        push_wide(ls.at[p], lg.at[p], 11 + p, False)
        lg[p, wide] = ls[p]
        rg[p, along] = rs[p]
        return carry

    lax.fori_loop(0, 2, forward_pair, 0)

    push_all(us, ur, 2)

    drain(gr, N_WIDE, recv.at[8])
    t32[...] = gr[...].astype(F32).reshape(2048, 128)

    for jn in range(32):
        from_j = (jn // 16 * 2 + jn % 2) * 8 + jn % 16 // 2
        part = jnp.concatenate(
            [t32[pl.ds(r * 32 + from_j, 16, stride=128), :] for r in range(RES)], axis=0
        ).astype(BF16)
        g2[jn, 0:64, 0:128] = part
        g2[jn, 64:128, 128:256] = part

    for at in range(8):
        res = nt(w2[...], g2[at * 4:at * 4 + 4].reshape(512, 256)).astype(BF16)
        for jj in range(4):
            for c_hi in range(16):
                y[at * 4 + jj, :, c_hi * 128:(c_hi + 1) * 128] = res[
                    c_hi * 32:(c_hi + 1) * 32, jj * 128:(jj + 1) * 128
                ]
    for r in range(RES):
        w_t[r] = w_all[r].astype(BF16).T

    for p in range(2):
        drain(lg.at[p], N_WIDE, recv.at[11 + p])
    t32[...] = lg[...].astype(F32).reshape(2048, 128)
    for c in range(32):
        part = jnp.concatenate(
            [
                t32[pl.ds((r // 2) * 1024 + (r % 2) * 32 + c, 16, stride=64), :]
                for r in range(RES)
            ],
            axis=0,
        )
        lp[c * 64:(c + 1) * 64, :] = part.astype(BF16)

    for p in range(2):
        res = nn(y[p * 16:(p + 1) * 16].reshape(512, 2048), lp[...]).astype(BF16)
        grs[p] = res.reshape(8, 64, 128)
    for p in range(2):
        grr[p, along] = grs[p, along]
        push_z(grs.at[p], grr.at[p], 19 + p, True)

    for p in range(2):
        drain(rg.at[p], N_Z, recv.at[15 + p])
    rg_t = rg[...].reshape(1024, 128).astype(F32).T.astype(BF16)
    for at in range(4):
        res = nn(rg_t, y[:, :, at * 512:(at + 1) * 512].reshape(1024, 512))
        t32[at * 512:(at + 1) * 512, :] = res.T
    for m in range(16):
        gls[m % 2, m // 2] = jnp.concatenate(
            [t32[pl.ds(m + 16 * r, 32, stride=64), :] for r in range(RES)], axis=0
        ).astype(BF16)
    pltpu.make_async_remote_copy(
        src_ref=gls.at[1 - core_here],
        dst_ref=glx,
        send_sem=send.at[24],
        recv_sem=recv.at[24],
        device_id={"dap": sibling},
        device_id_type=MESH,
    ).start()

    for group in range(4):
        if group == 2:
            pltpu.make_async_copy(glx, glx, recv.at[24]).wait()
            glo[...] = (gls[core_here].astype(F32) + glx[...].astype(F32)).astype(BF16)
            glr[level] = glo[level]
            push(level_group, glo, glr, send.at[23], recv.at[23], True)
        res = nt(rg[...].reshape(1024, 128), lp[group * 512:(group + 1) * 512, :]).astype(BF16)
        for jn in range(32):
            for cc in range(4):
                c_hi = group * 4 + cc
                xp[c_hi * 32:(c_hi + 1) * 32, jn * 128:(jn + 1) * 128] = res[
                    jn * 32:(jn + 1) * 32, cc * 128:(cc + 1) * 128
                ]
    pacc[...] = nn(xp[...], g2[...].reshape(4096, 256))

    for m in range(16):
        part = pacc[m * 32:(m + 1) * 32, :] * (1.0 / SEQ)
        ps[m] = jnp.concatenate([part[:, 0:128], part[:, 128:256]], axis=0).astype(BF16)
    pr[wide] = ps[wide]
    push_wide(ps, pr, 27, True)

    for p in range(2):
        drain(grr.at[p], N_Z, recv.at[19 + p])
    right_sum = jnp.sum(grr[...].astype(F32), axis=1).reshape(128, SEQ)
    drain(glr, N_Z, recv.at[23])
    left_sum = jnp.sum(glr[...].astype(F32), axis=0)
    owg = jnp.zeros((64, CH), F32)
    for r in range(RES):
        both = jnp.concatenate(
            [left_sum[r * 32:(r + 1) * 32, :], right_sum[r * 32:(r + 1) * 32, :]], axis=0
        )
        owg = owg + nn(both.astype(BF16), nmid[r])
        dcat[r] = both.T.astype(BF16)

    for m in range(16):
        half = m // 8
        qs[m] = jnp.concatenate(
            [
                owg[(m % 8) * 8:(m % 8) * 8 + 8, half * 128:(half + 1) * 128],
                jnp.zeros((8, 128), F32),
            ],
            axis=0,
        ).astype(BF16)
    qr[wide] = qs[wide]
    push_wide(qs, qr, 38, True)

    drain(ur, N_DAP, recv.at[2])
    t32[1024:2048, :] = ur[...].astype(F32).reshape(1024, 128)

    def backward(r, n):
        grad = nn(dcat[r], wf_ref[...]).astype(BF16).astype(F32)
        dmid = standardize_back(grad, hat_mid[r], sc_mid[r][:, 0:1]).astype(BF16).astype(F32)
        arriving = jnp.concatenate(
            [t32[pl.ds(1024 + 2 * r + half, SEQ, stride=8), :] for half in range(2)], axis=1
        )
        gm16 = (arriving + dmid).astype(BF16)
        gm = gm16.astype(F32)
        dgated = nt(gm16, wo_ref[...]).astype(BF16).astype(F32)
        g = gate[r]
        datt = blocks((dgated * g).astype(BF16))
        dpre = (dgated * att[r] * g * (1.0 - g)).astype(BF16)
        w = w_all[r]
        dw = nt(datt, v_all[r])
        ds = w * (dw - jnp.sum(w * dw, axis=-1, keepdims=True))
        dq = nn(side_by_side(ds.astype(BF16)), blocks(k_all[r])).astype(BF16)
        dq = (dq.astype(F32) * HEAD_DIM ** (-0.5)).astype(BF16)
        dk = nn(ds.T.astype(BF16), blocks(q_all[r])).astype(BF16)
        dv = nn(w_t[r], datt).astype(BF16)
        dnorm = (
            nt(dq, wq_ref[...]) + nt(dk, wk_ref[...]) + nt(dv, wv_ref[...]) + nt(dpre, wg_ref[...])
        ).astype(BF16).astype(F32)
        dx = standardize_back(dnorm, hat_in[r], sc_in[r][:, 0:1]).astype(BF16).astype(F32)
        total = gm + dx
        for half in range(2):
            u32[pl.ds(2 * n + half, SEQ, stride=4), :] = total[:, half * 128:(half + 1) * 128]

    def send_pair(p):
        os[p] = u32[0:512, :].reshape(N_DAP, 4, 128).astype(BF16)
        orr[p, me] = os[p, me]
        push_all(os.at[p], orr.at[p], 3 + p)

    for n in range(2):
        backward(n, n)

    drain(pr, N_WIDE, recv.at[27])
    zs[...] = jnp.sum(pr[...].astype(F32), axis=0).astype(BF16)
    zr[along] = zs[...]
    push_z(zs, zr, 28, False)
    send_pair(0)

    for n in range(2):
        backward(2 + n, n)
    drain(qr, N_WIDE, recv.at[38])
    zq[...] = jnp.sum(qr[...].astype(F32), axis=0).astype(BF16)
    zqr[along] = zq[...]
    push_z(zq, zqr, 39, False)
    send_pair(1)

    drain(zr, N_Z, recv.at[28])
    fs[...] = jnp.sum(zr[...].astype(F32), axis=0).astype(BF16)
    fr[wide] = fs[...]
    push_wide(fs, fr, 29, False)
    drain(zqr, N_Z, recv.at[39])
    fq[...] = jnp.sum(zqr[...].astype(F32), axis=0).astype(BF16)
    fqr[wide] = fq[...]
    push_wide(fq, fqr, 40, False)

    rfg_ref[...] = right_sum
    drain(xr.at[0], N_DAP, send.at[0])
    drain(xr.at[1], N_DAP, send.at[1])
    drain(ur, N_DAP, send.at[2])
    for p in range(2):
        drain(lg.at[p], N_WIDE, send.at[11 + p])
        drain(rg.at[p], N_Z, send.at[15 + p])
        drain(grr.at[p], N_Z, send.at[19 + p])
    drain(glr, N_Z, send.at[23])
    pltpu.make_async_copy(glx, glx, send.at[24]).wait()
    drain(gr, N_WIDE, send.at[8])
    drain(pr, N_WIDE, send.at[27])
    drain(qr, N_WIDE, send.at[38])
    drain(zr, N_Z, send.at[28])
    drain(zqr, N_Z, send.at[39])

    drain(fr, N_WIDE, recv.at[29])
    drain(fqr, N_WIDE, recv.at[40])
    halves = []
    for m in range(16):
        pwg_ref[m * 64:(m + 1) * 64, :] = fr[m].astype(F32)
        halves.append(fqr[m].astype(F32)[0:8, :])
    owg_ref[...] = jnp.concatenate(
        [jnp.concatenate(halves[0:8], axis=0), jnp.concatenate(halves[8:16], axis=0)], axis=1
    )
    drain(fr, N_WIDE, send.at[29])
    drain(fqr, N_WIDE, send.at[40])

    for p in range(2):
        drain(orr.at[p], N_DAP, recv.at[3 + p])
        t32[0:512, :] = orr[p].astype(F32).reshape(512, 128)
        for k in range(4):
            u32[pl.ds(4 * p + k, N_DAP, stride=8), :] = t32[pl.ds(k, N_DAP, stride=4), :]
    out_ref[:, 0:128] = u32[pl.ds(0, 512, stride=2), :].astype(BF16)
    out_ref[:, 128:256] = u32[pl.ds(1, 512, stride=2), :].astype(BF16)
    drain(orr.at[0], N_DAP, send.at[3])
    drain(orr.at[1], N_DAP, send.at[4])


def settle(*refs):
    found, results, sems = refs[0:4], refs[4:8], refs[8]
    copies = [pltpu.make_async_copy(found[n], results[n], sems.at[n]) for n in range(4)]
    for copy in copies:
        copy.start()
    for copy in copies:
        copy.wait()


SCRATCH = (
    [((512, CH), BF16)]
    + [((CH, CH), BF16)] * 4
    + [((1, CH), F32), ((CH, CH), BF16), ((64, CH), BF16), ((1024, 128), BF16)]
    + [((512, CH), BF16), ((2048, 128), BF16)]
    + [((2, N_DAP, 4, 128), BF16)] * 2
    + [((N_DAP, 8, 128), BF16)] * 2
    + [((16, 128, 128), BF16)] * 2
    + [((2048, 128), F32), ((1024, 128), F32)]
    + [((RES, SEQ, CH), F32)]
    + [((RES, SEQ, 128), F32)]
    + [((RES, SEQ, CH), F32)] * 2
    + [((RES, SEQ, CH), BF16)] * 3
    + [((RES, HEADS * SEQ, SEQ), F32)]
    + [((RES, SEQ, CH), BF16)]
    + [((RES, SEQ, CH), F32)]
    + [((RES, SEQ, 128), F32)]
    + [((2, 64, 128), BF16), ((2, 16, 64, 128), BF16)]
    + [((2, 64, 128), BF16), ((2, 8, 64, 128), BF16)]
    + [((2048, 128), BF16)]
    + [((32, 128, 256), BF16)]
    + [((512, 256), BF16)]
    + [((32, 32, 2048), BF16)]
    + [((512, 4096), BF16)]
    + [((512, 256), F32)]
    + [((2, 8, 128, 128), BF16)]
    + [((8, 128, 128), BF16)] * 3
    + [((2, 8, 64, 128), BF16)] * 2
    + [((RES, SEQ, 64), BF16)]
    + [((16, 64, 128), BF16)] * 2
    + [((16, 16, 128), BF16)] * 2
    + [((64, 128), BF16), ((8, 64, 128), BF16)]
    + [((16, 128), BF16), ((8, 16, 128), BF16)]
    + [((64, 128), BF16), ((16, 64, 128), BF16)]
    + [((16, 128), BF16), ((16, 16, 128), BF16)]
    + [((2, N_DAP, 4, 128), BF16)] * 2
    + [((RES, SEQ, HEADS * SEQ), BF16)]
)
SEMAPHORES = 41


def body(
    aligned_rows,
    asking_projection,
    lookup_projection,
    content_projection,
    sigmoid_projection,
    sigmoid_shift,
    result_projection,
    tensor_mean_projections,
    twofold_projection,
    refreshed_rows_adjoint,
    twofold_change_adjoint,
):
    whole = pl.BlockSpec(memory_space=pltpu.VMEM)
    anywhere = pl.BlockSpec(memory_space=pl.ANY)
    results = (
        jax.ShapeDtypeStruct((512, CH), BF16),
        jax.ShapeDtypeStruct((1024, 128), F32),
        jax.ShapeDtypeStruct((64, CH), F32),
        jax.ShapeDtypeStruct((128, SEQ), F32),
    )
    found = pl.pallas_call(
        kernel,
        out_shape=tuple(pltpu.VMEM(result.shape, result.dtype) for result in results),
        in_specs=[anywhere] * 11,
        out_specs=(whole,) * 4,
        scratch_shapes=[pltpu.VMEM(shape, kind) for shape, kind in SCRATCH]
        + [pltpu.SemaphoreType.DMA((SEMAPHORES,)), pltpu.SemaphoreType.DMA((SEMAPHORES,))]
        + [pltpu.SemaphoreType.DMA((11,))],
        compiler_params=pltpu.CompilerParams(
            collective_id=0, has_side_effects=True, vmem_limit_bytes=56 * 2**20
        ),
        name="evoformer_backward",
    )(
        aligned_rows.reshape(512, CH),
        asking_projection,
        lookup_projection,
        content_projection,
        sigmoid_projection,
        sigmoid_shift.reshape(1, CH),
        result_projection,
        tensor_mean_projections.T,
        twofold_projection,
        refreshed_rows_adjoint.reshape(512, CH),
        twofold_change_adjoint.reshape(2048, 128),
    )
    out, pwg, owg, rfg = pl.pallas_call(
        settle,
        out_shape=results,
        in_specs=[anywhere] * 4,
        out_specs=(anywhere,) * 4,
        scratch_shapes=[pltpu.SemaphoreType.DMA((4,))],
        name="settle",
    )(*[pltpu.with_memory_space_constraint(array, pltpu.VMEM) for array in found])
    return (
        out.reshape(1, 512, CH),
        pwg,
        owg.T,
        rfg.reshape(RES, 32, SEQ).transpose(2, 0, 1),
    )


def solution(mesh):
    split = P(("dp", "dap"), None, None)
    in_specs = (split,) + (P(),) * 8 + (split, split)
    out_specs = (split, P("dp", None), P("dp", None), P("dp", "dap", None))
    return jax.shard_map(body, mesh=mesh, in_specs=in_specs, out_specs=out_specs, check_vma=False)
```

```python
import functools

import jax
import jax.numpy as jnp
from jax import lax
from jax.experimental import pallas as pl
from jax.experimental.pallas import tpu as pltpu
from jax.sharding import PartitionSpec as P

HEADS = 8
HEAD_DIM = 32
SEQ = 128
RES = 4
CH = 256
N_DAP = 128
N_WIDE = 16
N_Z = 8
MESH = pl.DeviceIdType.MESH
F32 = jnp.float32
BF16 = jnp.bfloat16


def nn(a, b):
    return lax.dot_general(a, b, (((1,), (0,)), ((), ())), preferred_element_type=F32)


def nt(a, b):
    return lax.dot_general(a, b, (((1,), (1,)), ((), ())), preferred_element_type=F32)


def far_first():
    steps = [
        (dx, dy, dz, dc)
        for dy in range(4) for dz in range(8) for dx in range(2) for dc in range(2)
        if dx or dy or dz or dc
    ]
    return sorted(steps, key=lambda d: -(2 * (d[0] + min(d[1], 4 - d[1]) + min(d[2], 8 - d[2])) + d[3]))


def groups(me):
    x = lax.div(me, 64)
    y = lax.rem(lax.div(me, 16), 4)
    z = lax.rem(lax.div(me, 2), 8)
    core = lax.rem(me, 2)
    step = 1 - 2 * core
    xs = [x * 64, (1 - x) * 64]
    ys = [lax.rem(y + 4 + d * step, 4) * 16 for d in range(4)]
    zs = [lax.rem(z + 8 + d * step, 8) for d in range(8)]
    twice = [place * 2 for place in zs]
    cores = [core, 1 - core]
    everyone = []
    for dx, dy, dz, dc in far_first():
        device = xs[dx] + ys[dy] + twice[dz] + cores[dc]
        everyone.append((device, device))
    wide = []
    for dx, dy, dc in (
        (1, 2, 0), (0, 2, 1), (1, 1, 0), (1, 3, 1), (1, 2, 1), (0, 2, 0), (1, 1, 1), (1, 3, 0),
        (0, 1, 0), (0, 3, 1), (1, 0, 0), (0, 1, 1), (0, 3, 0), (1, 0, 1), (0, 0, 1),
    ):
        line = xs[dx] + ys[dy]
        wide.append((line + z * 2 + cores[dc], lax.div(line, 8) + cores[dc]))
    long = [(xs[0] + ys[0] + twice[dz] + core, zs[dz]) for dz in (4, 3, 5, 2, 6, 1, 7)]
    level = []
    for dx, dy in ((1, 2), (0, 2), (1, 1), (1, 3), (0, 1), (0, 3), (1, 0)):
        line = xs[dx] + ys[dy]
        level.append((line + z * 2 + core, lax.div(line, 16)))
    line = xs[0] + ys[0]
    return (
        (me, everyone),
        (lax.div(line, 8) + core, wide),
        (z, long),
        (lax.div(line, 16), level),
        line + z * 2 + 1 - core,
    )


def push(group, sample, src, dst, send_sem, recv_sem, spread):
    mine, others = group
    for device, place in others:
        pltpu.make_async_remote_copy(
            src_ref=src.at[place] if spread else src,
            dst_ref=dst.at[mine],
            send_sem=send_sem,
            recv_sem=recv_sem,
            device_id=(device, sample),
            device_id_type=MESH,
        ).start()


def drain(ref, total, sem):
    part = ref.at[pl.ds(0, total - 1)]
    pltpu.make_async_copy(part, part, sem).wait()


def standardize(wide):
    average = jnp.mean(wide, axis=-1, keepdims=True)
    centred = wide - average
    variance = jnp.mean(centred * centred, axis=-1, keepdims=True)
    scale = lax.rsqrt(variance + 1e-05)
    return centred * scale, scale


def standardize_back(grad, hat, scale):
    return scale * (
        grad
        - jnp.mean(grad, axis=-1, keepdims=True)
        - hat * jnp.mean(grad * hat, axis=-1, keepdims=True)
    )


def kernel(
    rows_in, wq_in, wk_in, wv_in, wg_in, shift_in, wo_in, wf_in, wp_in, adj_in, pair_in,
    out_ref, pwg_ref, owg_ref, rfg_ref,
    rows_ref, wq_ref, wk_ref, wv_ref, wg_ref, shift_ref, wo_ref, wf_ref, wp_ref, adj_ref, pair_ref,
    xs, xr, us, ur, gs, gr, t32, u32, hat_in, sc_in, gate, att, q_all, k_all,
    v_all, w_all, nmid, hat_mid, sc_mid, ls, lg, rs, rg, lp, g2, w2, y, xp, pacc, gls, glx, glo, glr, grs, grr,
    dcat, ps, pr, qs, qr, zs, zr, zq, zqr, fs, fr, fq, fqr, os, orr, w_t, send, recv, bring,
):
    me = lax.axis_index("dap")
    sample = lax.axis_index("dp")
    whole_group, wide_group, long_group, level_group, sibling = groups(me)
    wide, along, level = wide_group[0], long_group[0], level_group[0]
    core_here = lax.rem(me, 2)
    pairs = (
        (rows_in, rows_ref), (pair_in, pair_ref), (adj_in, adj_ref), (wp_in, wp_ref), (wq_in, wq_ref),
        (wk_in, wk_ref), (wv_in, wv_ref), (wg_in, wg_ref), (shift_in, shift_ref), (wo_in, wo_ref),
        (wf_in, wf_ref),
    )
    brought = [pltpu.make_async_copy(a, b, bring.at[n]) for n, (a, b) in enumerate(pairs)]
    for copy in brought:
        copy.start()
    bar = pltpu.get_barrier_semaphore()
    for device, _ in whole_group[1]:
        pl.semaphore_signal(bar, inc=1, device_id=(device, sample), device_id_type=MESH)

    def push_all(src, dst, sem):
        push(whole_group, sample, src, dst, send.at[sem], recv.at[sem], True)

    def push_wide(src, dst, sem, spread):
        push(wide_group, sample, src, dst, send.at[sem], recv.at[sem], spread)

    def push_z(src, dst, sem, spread):
        push(long_group, sample, src, dst, send.at[sem], recv.at[sem], spread)

    def stage_rows(ref):
        u32[pl.ds(0, 512, stride=2), :] = ref[:, 0:128].astype(F32)
        u32[pl.ds(1, 512, stride=2), :] = ref[:, 128:256].astype(F32)

    brought[0].wait()
    stage_rows(rows_ref)
    for p in range(2):
        xs[p] = u32[...].reshape(N_DAP, 8, 128)[:, 4 * p:4 * p + 4, :].astype(BF16)
        xr[p, me] = xs[p, me]
    pl.semaphore_wait(bar, N_DAP - 1)

    for p in range(2):
        push_all(xs.at[p], xr.at[p], p)

    brought[1].wait()
    t32[...] = pair_ref[...].astype(F32)

    def stage_pair(at, carry):
        for core in range(2):
            for i in range(RES):
                parts = [
                    t32[pl.ds(i * 512 + at * 64 + core * 4 + r, 8, stride=8), :] for r in range(RES)
                ]
                gs[at * 2 + core, i * 32:(i + 1) * 32, :] = jnp.concatenate(parts, axis=0).astype(BF16)
        return carry

    lax.fori_loop(0, 8, stage_pair, 0)
    gr[wide] = gs[wide]
    push_wide(gs, gr, 8, True)

    for copy in brought[2:]:
        copy.wait()
    stage_rows(adj_ref)
    us[...] = u32[...].reshape(N_DAP, 8, 128).astype(BF16)
    ur[me] = us[me]
    g2[...] = jnp.zeros_like(g2)
    for c_hi in range(16):
        for c_lo in range(2):
            w2[c_hi * 32:(c_hi + 1) * 32, c_lo * 128:(c_lo + 1) * 128] = (
                wp_ref[(2 * c_hi + c_lo) * 32:(2 * c_hi + c_lo + 1) * 32, :].astype(F32) * (1.0 / SEQ)
            ).astype(BF16)

    lane_head = lax.broadcasted_iota(jnp.int32, (1, CH), 1) // HEAD_DIM
    masks = [(lane_head == h).astype(F32).astype(BF16) for h in range(HEADS)]

    def blocks(value):
        return jnp.concatenate([value * m for m in masks], axis=0)

    def side_by_side(value):
        return jnp.concatenate([value[h * 128:(h + 1) * 128, :] for h in range(HEADS)], axis=1)

    def forward(r, n):
        x = jnp.concatenate(
            [u32[pl.ds(2 * n + half, SEQ, stride=4), :] for half in range(2)], axis=1
        )
        hat, scale = standardize(x)
        hat_in[r] = hat
        sc_in[r] = jnp.broadcast_to(scale, (SEQ, 128))
        normed = hat.astype(BF16)
        q = (nn(normed, wq_ref[...]) * HEAD_DIM ** (-0.5)).astype(BF16)
        k = nn(normed, wk_ref[...]).astype(BF16)
        v = nn(normed, wv_ref[...]).astype(BF16)
        g = jax.nn.sigmoid(nn(normed, wg_ref[...]) + shift_ref[...])
        q_all[r] = q
        k_all[r] = k
        v_all[r] = v
        gate[r] = g
        scores = nt(blocks(q), k)
        e = jnp.exp(scores - jnp.max(scores, axis=-1, keepdims=True))
        w = e * (1.0 / jnp.sum(e, axis=-1, keepdims=True))
        w_all[r] = w
        a = nn(side_by_side(w.astype(BF16)), blocks(v))
        att[r] = a
        gated = (a * g).astype(BF16)
        upd = (x + nn(gated, wo_ref[...])).astype(BF16).astype(F32)
        hat, scale = standardize(upd)
        hat_mid[r] = hat
        sc_mid[r] = jnp.broadcast_to(scale, (SEQ, 128))
        normed = hat.astype(BF16)
        nmid[r] = normed
        factors = nt(wf_ref[...], normed).astype(BF16)
        return factors

    def forward_pair(p, carry):
        drain(xr.at[p], N_DAP, recv.at[p])
        u32[0:512, :] = xr[p].astype(F32).reshape(512, 128)
        both = [forward(2 * p + n, n) for n in range(2)]
        ls[p] = jnp.concatenate([factors[0:32, :] for factors in both], axis=0)
        rs[p] = jnp.concatenate([factors[32:64, :] for factors in both], axis=0)
        push_z(rs.at[p], rg.at[p], 15 + p, False)
        push_wide(ls.at[p], lg.at[p], 11 + p, False)
        lg[p, wide] = ls[p]
        rg[p, along] = rs[p]
        return carry

    lax.fori_loop(0, 2, forward_pair, 0)

    push_all(us, ur, 2)

    drain(gr, N_WIDE, recv.at[8])
    t32[...] = gr[...].astype(F32).reshape(2048, 128)

    for jn in range(32):
        from_j = (jn // 16 * 2 + jn % 2) * 8 + jn % 16 // 2
        part = jnp.concatenate(
            [t32[pl.ds(r * 32 + from_j, 16, stride=128), :] for r in range(RES)], axis=0
        ).astype(BF16)
        g2[jn, 0:64, 0:128] = part
        g2[jn, 64:128, 128:256] = part

    for at in range(8):
        res = nt(w2[...], g2[at * 4:at * 4 + 4].reshape(512, 256)).astype(BF16)
        for jj in range(4):
            for c_hi in range(16):
                y[at * 4 + jj, :, c_hi * 128:(c_hi + 1) * 128] = res[
                    c_hi * 32:(c_hi + 1) * 32, jj * 128:(jj + 1) * 128
                ]
    for r in range(RES):
        w_t[r] = w_all[r].astype(BF16).T

    for p in range(2):
        drain(lg.at[p], N_WIDE, recv.at[11 + p])
    t32[...] = lg[...].astype(F32).reshape(2048, 128)
    for c in range(32):
        part = jnp.concatenate(
            [
                t32[pl.ds((r // 2) * 1024 + (r % 2) * 32 + c, 16, stride=64), :]
                for r in range(RES)
            ],
            axis=0,
        )
        lp[c * 64:(c + 1) * 64, :] = part.astype(BF16)

    for p in range(2):
        res = nn(y[p * 16:(p + 1) * 16].reshape(512, 2048), lp[...]).astype(BF16)
        grs[p] = res.reshape(8, 64, 128)
    for p in range(2):
        grr[p, along] = grs[p, along]
        push_z(grs.at[p], grr.at[p], 19 + p, True)

    for p in range(2):
        drain(rg.at[p], N_Z, recv.at[15 + p])
    rg_t = rg[...].reshape(1024, 128).astype(F32).T.astype(BF16)
    for at in range(4):
        res = nn(rg_t, y[:, :, at * 512:(at + 1) * 512].reshape(1024, 512))
        t32[at * 512:(at + 1) * 512, :] = res.T
    for m in range(16):
        gls[m % 2, m // 2] = jnp.concatenate(
            [t32[pl.ds(m + 16 * r, 32, stride=64), :] for r in range(RES)], axis=0
        ).astype(BF16)
    pltpu.make_async_remote_copy(
        src_ref=gls.at[1 - core_here],
        dst_ref=glx,
        send_sem=send.at[24],
        recv_sem=recv.at[24],
        device_id=(sibling, sample),
        device_id_type=MESH,
    ).start()

    for group in range(4):
        if group == 2:
            pltpu.make_async_copy(glx, glx, recv.at[24]).wait()
            glo[...] = (gls[core_here].astype(F32) + glx[...].astype(F32)).astype(BF16)
            glr[level] = glo[level]
            push(level_group, sample, glo, glr, send.at[23], recv.at[23], True)
        res = nt(rg[...].reshape(1024, 128), lp[group * 512:(group + 1) * 512, :]).astype(BF16)
        for jn in range(32):
            for cc in range(4):
                c_hi = group * 4 + cc
                xp[c_hi * 32:(c_hi + 1) * 32, jn * 128:(jn + 1) * 128] = res[
                    jn * 32:(jn + 1) * 32, cc * 128:(cc + 1) * 128
                ]
    pacc[...] = nn(xp[...], g2[...].reshape(4096, 256))

    for m in range(16):
        part = pacc[m * 32:(m + 1) * 32, :] * (1.0 / SEQ)
        ps[m] = jnp.concatenate([part[:, 0:128], part[:, 128:256]], axis=0).astype(BF16)
    pr[wide] = ps[wide]
    push_wide(ps, pr, 27, True)

    for p in range(2):
        drain(grr.at[p], N_Z, recv.at[19 + p])
    right_sum = jnp.sum(grr[...].astype(F32), axis=1).reshape(128, SEQ)
    drain(glr, N_Z, recv.at[23])
    left_sum = jnp.sum(glr[...].astype(F32), axis=0)
    owg = jnp.zeros((64, CH), F32)
    for r in range(RES):
        both = jnp.concatenate(
            [left_sum[r * 32:(r + 1) * 32, :], right_sum[r * 32:(r + 1) * 32, :]], axis=0
        )
        owg = owg + nn(both.astype(BF16), nmid[r])
        dcat[r] = both.T.astype(BF16)

    for m in range(16):
        half = m // 8
        qs[m] = jnp.concatenate(
            [
                owg[(m % 8) * 8:(m % 8) * 8 + 8, half * 128:(half + 1) * 128],
                jnp.zeros((8, 128), F32),
            ],
            axis=0,
        ).astype(BF16)
    qr[wide] = qs[wide]
    push_wide(qs, qr, 38, True)

    drain(ur, N_DAP, recv.at[2])
    t32[1024:2048, :] = ur[...].astype(F32).reshape(1024, 128)

    def backward(r, n):
        grad = nn(dcat[r], wf_ref[...]).astype(BF16).astype(F32)
        dmid = standardize_back(grad, hat_mid[r], sc_mid[r][:, 0:1]).astype(BF16).astype(F32)
        arriving = jnp.concatenate(
            [t32[pl.ds(1024 + 2 * r + half, SEQ, stride=8), :] for half in range(2)], axis=1
        )
        gm16 = (arriving + dmid).astype(BF16)
        gm = gm16.astype(F32)
        dgated = nt(gm16, wo_ref[...]).astype(BF16).astype(F32)
        g = gate[r]
        datt = blocks((dgated * g).astype(BF16))
        dpre = (dgated * att[r] * g * (1.0 - g)).astype(BF16)
        w = w_all[r]
        dw = nt(datt, v_all[r])
        ds = w * (dw - jnp.sum(w * dw, axis=-1, keepdims=True))
        dq = nn(side_by_side(ds.astype(BF16)), blocks(k_all[r])).astype(BF16)
        dq = (dq.astype(F32) * HEAD_DIM ** (-0.5)).astype(BF16)
        dk = nn(ds.T.astype(BF16), blocks(q_all[r])).astype(BF16)
        dv = nn(w_t[r], datt).astype(BF16)
        dnorm = (
            nt(dq, wq_ref[...]) + nt(dk, wk_ref[...]) + nt(dv, wv_ref[...]) + nt(dpre, wg_ref[...])
        ).astype(BF16).astype(F32)
        dx = standardize_back(dnorm, hat_in[r], sc_in[r][:, 0:1]).astype(BF16).astype(F32)
        total = gm + dx
        for half in range(2):
            u32[pl.ds(2 * r + half, SEQ, stride=8), :] = total[:, half * 128:(half + 1) * 128]

    def send_pair(p):
        if p == 1:
            os[...] = u32[...].reshape(N_DAP, 8, 128).astype(BF16)
            orr[me] = os[me]
            push_all(os, orr, 3)

    for n in range(2):
        backward(n, n)

    drain(pr, N_WIDE, recv.at[27])
    zs[...] = jnp.sum(pr[...].astype(F32), axis=0).astype(BF16)
    zr[along] = zs[...]
    push_z(zs, zr, 28, False)
    send_pair(0)

    for n in range(2):
        backward(2 + n, n)
    drain(qr, N_WIDE, recv.at[38])
    zq[...] = jnp.sum(qr[...].astype(F32), axis=0).astype(BF16)
    zqr[along] = zq[...]
    push_z(zq, zqr, 39, False)
    send_pair(1)

    drain(zr, N_Z, recv.at[28])
    fs[...] = jnp.sum(zr[...].astype(F32), axis=0).astype(BF16)
    fr[wide] = fs[...]
    push_wide(fs, fr, 29, False)
    drain(zqr, N_Z, recv.at[39])
    fq[...] = jnp.sum(zqr[...].astype(F32), axis=0).astype(BF16)
    fqr[wide] = fq[...]
    push_wide(fq, fqr, 40, False)

    rfg_ref[...] = right_sum
    drain(xr.at[0], N_DAP, send.at[0])
    drain(xr.at[1], N_DAP, send.at[1])
    drain(ur, N_DAP, send.at[2])
    for p in range(2):
        drain(lg.at[p], N_WIDE, send.at[11 + p])
        drain(rg.at[p], N_Z, send.at[15 + p])
        drain(grr.at[p], N_Z, send.at[19 + p])
    drain(glr, N_Z, send.at[23])
    pltpu.make_async_copy(glx, glx, send.at[24]).wait()
    drain(gr, N_WIDE, send.at[8])
    drain(pr, N_WIDE, send.at[27])
    drain(qr, N_WIDE, send.at[38])
    drain(zr, N_Z, send.at[28])
    drain(zqr, N_Z, send.at[39])

    drain(fr, N_WIDE, recv.at[29])
    drain(fqr, N_WIDE, recv.at[40])
    halves = []
    for m in range(16):
        pwg_ref[m * 64:(m + 1) * 64, :] = fr[m].astype(F32)
        halves.append(fqr[m].astype(F32)[0:8, :])
    owg_ref[...] = jnp.concatenate(
        [jnp.concatenate(halves[0:8], axis=0), jnp.concatenate(halves[8:16], axis=0)], axis=1
    )
    drain(fr, N_WIDE, send.at[29])
    drain(fqr, N_WIDE, send.at[40])

    drain(orr, N_DAP, recv.at[3])
    u32[...] = orr[...].astype(F32).reshape(1024, 128)
    out_ref[:, 0:128] = u32[pl.ds(0, 512, stride=2), :].astype(BF16)
    out_ref[:, 128:256] = u32[pl.ds(1, 512, stride=2), :].astype(BF16)
    drain(orr, N_DAP, send.at[3])


def settle(*refs):
    found, results, sems = refs[0:4], refs[4:8], refs[8]
    copies = [pltpu.make_async_copy(found[n], results[n], sems.at[n]) for n in range(4)]
    for copy in copies:
        copy.start()
    for copy in copies:
        copy.wait()


SCRATCH = (
    [((512, CH), BF16)]
    + [((CH, CH), BF16)] * 4
    + [((1, CH), F32), ((CH, CH), BF16), ((64, CH), BF16), ((1024, 128), BF16)]
    + [((512, CH), BF16), ((2048, 128), BF16)]
    + [((2, N_DAP, 4, 128), BF16)] * 2
    + [((N_DAP, 8, 128), BF16)] * 2
    + [((16, 128, 128), BF16)] * 2
    + [((2048, 128), F32), ((1024, 128), F32)]
    + [((RES, SEQ, CH), F32)]
    + [((RES, SEQ, 128), F32)]
    + [((RES, SEQ, CH), F32)] * 2
    + [((RES, SEQ, CH), BF16)] * 3
    + [((RES, HEADS * SEQ, SEQ), F32)]
    + [((RES, SEQ, CH), BF16)]
    + [((RES, SEQ, CH), F32)]
    + [((RES, SEQ, 128), F32)]
    + [((2, 64, 128), BF16), ((2, 16, 64, 128), BF16)]
    + [((2, 64, 128), BF16), ((2, 8, 64, 128), BF16)]
    + [((2048, 128), BF16)]
    + [((32, 128, 256), BF16)]
    + [((512, 256), BF16)]
    + [((32, 32, 2048), BF16)]
    + [((512, 4096), BF16)]
    + [((512, 256), F32)]
    + [((2, 8, 128, 128), BF16)]
    + [((8, 128, 128), BF16)] * 3
    + [((2, 8, 64, 128), BF16)] * 2
    + [((RES, SEQ, 64), BF16)]
    + [((16, 64, 128), BF16)] * 2
    + [((16, 16, 128), BF16)] * 2
    + [((64, 128), BF16), ((8, 64, 128), BF16)]
    + [((16, 128), BF16), ((8, 16, 128), BF16)]
    + [((64, 128), BF16), ((16, 64, 128), BF16)]
    + [((16, 128), BF16), ((16, 16, 128), BF16)]
    + [((N_DAP, 8, 128), BF16)] * 2
    + [((RES, SEQ, HEADS * SEQ), BF16)]
)
SEMAPHORES = 41


def body(
    aligned_rows,
    asking_projection,
    lookup_projection,
    content_projection,
    sigmoid_projection,
    sigmoid_shift,
    result_projection,
    tensor_mean_projections,
    twofold_projection,
    refreshed_rows_adjoint,
    twofold_change_adjoint,
):
    whole = pl.BlockSpec(memory_space=pltpu.VMEM)
    anywhere = pl.BlockSpec(memory_space=pl.ANY)
    results = (
        jax.ShapeDtypeStruct((512, CH), BF16),
        jax.ShapeDtypeStruct((1024, 128), F32),
        jax.ShapeDtypeStruct((64, CH), F32),
        jax.ShapeDtypeStruct((128, SEQ), F32),
    )
    found = pl.pallas_call(
        kernel,
        out_shape=tuple(pltpu.VMEM(result.shape, result.dtype) for result in results),
        in_specs=[anywhere] * 11,
        out_specs=(whole,) * 4,
        scratch_shapes=[pltpu.VMEM(shape, kind) for shape, kind in SCRATCH]
        + [pltpu.SemaphoreType.DMA((SEMAPHORES,)), pltpu.SemaphoreType.DMA((SEMAPHORES,))]
        + [pltpu.SemaphoreType.DMA((11,))],
        compiler_params=pltpu.CompilerParams(
            collective_id=0, has_side_effects=True, vmem_limit_bytes=56 * 2**20
        ),
        name="evoformer_backward",
    )(
        aligned_rows.reshape(512, CH),
        asking_projection,
        lookup_projection,
        content_projection,
        sigmoid_projection,
        sigmoid_shift.reshape(1, CH),
        result_projection,
        tensor_mean_projections.T,
        twofold_projection,
        refreshed_rows_adjoint.reshape(512, CH),
        twofold_change_adjoint.reshape(2048, 128),
    )
    out, pwg, owg, rfg = pl.pallas_call(
        settle,
        out_shape=results,
        in_specs=[anywhere] * 4,
        out_specs=(anywhere,) * 4,
        scratch_shapes=[pltpu.SemaphoreType.DMA((4,))],
        name="settle",
    )(*[pltpu.with_memory_space_constraint(array, pltpu.VMEM) for array in found])
    return (
        out.reshape(1, 512, CH),
        pwg,
        owg.T,
        rfg.reshape(RES, 32, SEQ).transpose(2, 0, 1),
    )


def solution(mesh):
    split = P(("dp", "dap"), None, None)
    in_specs = (split,) + (P(),) * 8 + (split, split)
    out_specs = (split, P("dp", None), P("dp", None), P("dp", "dap", None))
    return jax.shard_map(body, mesh=mesh, in_specs=in_specs, out_specs=out_specs, check_vma=False)
```

```python
import functools

import jax
import jax.numpy as jnp
from jax import lax
from jax.experimental import pallas as pl
from jax.experimental.pallas import tpu as pltpu
from jax.sharding import PartitionSpec as P

HEADS = 8
HEAD_DIM = 32
SEQ = 128
RES = 4
CH = 256
N_DAP = 128
N_WIDE = 16
N_Z = 8
MESH = pl.DeviceIdType.MESH
F32 = jnp.float32
BF16 = jnp.bfloat16


def nn(a, b):
    return lax.dot_general(a, b, (((1,), (0,)), ((), ())), preferred_element_type=F32)


def nt(a, b):
    return lax.dot_general(a, b, (((1,), (1,)), ((), ())), preferred_element_type=F32)


def far_first():
    steps = [
        (dx, dy, dz, dc)
        for dy in range(4) for dz in range(8) for dx in range(2) for dc in range(2)
        if dx or dy or dz or dc
    ]
    return sorted(steps, key=lambda d: -(2 * (d[0] + min(d[1], 4 - d[1]) + min(d[2], 8 - d[2])) + d[3]))


def groups(me):
    x = lax.div(me, 64)
    y = lax.rem(lax.div(me, 16), 4)
    z = lax.rem(lax.div(me, 2), 8)
    core = lax.rem(me, 2)
    step = 1 - 2 * core
    xs = [x * 64, (1 - x) * 64]
    ys = [lax.rem(y + 4 + d * step, 4) * 16 for d in range(4)]
    zs = [lax.rem(z + 8 + d * step, 8) for d in range(8)]
    twice = [place * 2 for place in zs]
    cores = [core, 1 - core]
    everyone = []
    for dx, dy, dz, dc in far_first():
        device = xs[dx] + ys[dy] + twice[dz] + cores[dc]
        everyone.append((device, device))
    wide = []
    for dx, dy, dc in (
        (1, 2, 0), (0, 2, 1), (1, 1, 0), (1, 3, 1), (1, 2, 1), (0, 2, 0), (1, 1, 1), (1, 3, 0),
        (0, 1, 0), (0, 3, 1), (1, 0, 0), (0, 1, 1), (0, 3, 0), (1, 0, 1), (0, 0, 1),
    ):
        line = xs[dx] + ys[dy]
        wide.append((line + z * 2 + cores[dc], lax.div(line, 8) + cores[dc]))
    long = [(xs[0] + ys[0] + twice[dz] + core, zs[dz]) for dz in (4, 3, 5, 2, 6, 1, 7)]
    level = []
    for dx, dy in ((1, 2), (0, 2), (1, 1), (1, 3), (0, 1), (0, 3), (1, 0)):
        line = xs[dx] + ys[dy]
        level.append((line + z * 2 + core, lax.div(line, 16)))
    line = xs[0] + ys[0]
    return (
        (me, everyone),
        (lax.div(line, 8) + core, wide),
        (z, long),
        (lax.div(line, 16), level),
        line + z * 2 + 1 - core,
    )


def push(group, sample, src, dst, send_sem, recv_sem, spread):
    mine, others = group
    for device, place in others:
        pltpu.make_async_remote_copy(
            src_ref=src.at[place] if spread else src,
            dst_ref=dst.at[mine],
            send_sem=send_sem,
            recv_sem=recv_sem,
            device_id=(device, sample),
            device_id_type=MESH,
        ).start()


def drain(ref, total, sem):
    part = ref.at[pl.ds(0, total - 1)]
    pltpu.make_async_copy(part, part, sem).wait()


def standardize(wide):
    average = jnp.mean(wide, axis=-1, keepdims=True)
    centred = wide - average
    variance = jnp.mean(centred * centred, axis=-1, keepdims=True)
    scale = lax.rsqrt(variance + 1e-05)
    return centred * scale, scale


def standardize_back(grad, hat, scale):
    return scale * (
        grad
        - jnp.mean(grad, axis=-1, keepdims=True)
        - hat * jnp.mean(grad * hat, axis=-1, keepdims=True)
    )


def kernel(
    rows_in, wq_in, wk_in, wv_in, wg_in, shift_in, wo_in, wf_in, wp_in, adj_in, pair_in,
    out_ref, pwg_ref, owg_ref, rfg_ref,
    rows_ref, wq_ref, wk_ref, wv_ref, wg_ref, shift_ref, wo_ref, wf_ref, wp_ref, adj_ref, pair_ref,
    xs, xr, us, ur, gs, gr, t32, u32, hat_in, sc_in, gate, att, q_all, k_all,
    v_all, w_all, nmid, hat_mid, sc_mid, ls, lg, rs, rg, lp, g2, w2, y, xp, pacc, gls, glx, glo, glr, grs, grr,
    dcat, ps, pr, qs, qr, zs, zr, zq, zqr, fs, fr, fq, fqr, os, orr, w_t, send, recv, bring,
):
    me = lax.axis_index("dap")
    sample = lax.axis_index("dp")
    whole_group, wide_group, long_group, level_group, sibling = groups(me)
    wide, along, level = wide_group[0], long_group[0], level_group[0]
    core_here = lax.rem(me, 2)
    pairs = (
        (rows_in, rows_ref), (pair_in, pair_ref), (adj_in, adj_ref), (wp_in, wp_ref), (wq_in, wq_ref),
        (wk_in, wk_ref), (wv_in, wv_ref), (wg_in, wg_ref), (shift_in, shift_ref), (wo_in, wo_ref),
        (wf_in, wf_ref),
    )
    brought = [pltpu.make_async_copy(a, b, bring.at[n]) for n, (a, b) in enumerate(pairs)]
    brought[0].start()
    bar = pltpu.get_barrier_semaphore()
    for device, _ in whole_group[1]:
        pl.semaphore_signal(bar, inc=1, device_id=(device, sample), device_id_type=MESH)

    for copy in brought[1:]:
        copy.start()

    def push_all(src, dst, sem):
        push(whole_group, sample, src, dst, send.at[sem], recv.at[sem], True)

    def push_wide(src, dst, sem, spread):
        push(wide_group, sample, src, dst, send.at[sem], recv.at[sem], spread)

    def push_z(src, dst, sem, spread):
        push(long_group, sample, src, dst, send.at[sem], recv.at[sem], spread)

    def stage_rows(ref):
        u32[pl.ds(0, 512, stride=2), :] = ref[:, 0:128].astype(F32)
        u32[pl.ds(1, 512, stride=2), :] = ref[:, 128:256].astype(F32)

    brought[0].wait()
    stage_rows(rows_ref)
    for p in range(2):
        xs[p] = u32[...].reshape(N_DAP, 8, 128)[:, 4 * p:4 * p + 4, :].astype(BF16)
        xr[p, me] = xs[p, me]
    pl.semaphore_wait(bar, N_DAP - 1)

    for p in range(2):
        push_all(xs.at[p], xr.at[p], p)

    brought[1].wait()
    t32[...] = pair_ref[...].astype(F32)

    def stage_pair(at, carry):
        for core in range(2):
            for i in range(RES):
                parts = [
                    t32[pl.ds(i * 512 + at * 64 + core * 4 + r, 8, stride=8), :] for r in range(RES)
                ]
                gs[at * 2 + core, i * 32:(i + 1) * 32, :] = jnp.concatenate(parts, axis=0).astype(BF16)
        return carry

    lax.fori_loop(0, 8, stage_pair, 0)
    gr[wide] = gs[wide]
    push_wide(gs, gr, 8, True)

    for copy in brought[2:]:
        copy.wait()
    stage_rows(adj_ref)
    us[...] = u32[...].reshape(N_DAP, 8, 128).astype(BF16)
    ur[me] = us[me]
    g2[...] = jnp.zeros_like(g2)
    for c_hi in range(16):
        for c_lo in range(2):
            w2[c_hi * 32:(c_hi + 1) * 32, c_lo * 128:(c_lo + 1) * 128] = (
                wp_ref[(2 * c_hi + c_lo) * 32:(2 * c_hi + c_lo + 1) * 32, :].astype(F32) * (1.0 / SEQ)
            ).astype(BF16)

    lane_head = lax.broadcasted_iota(jnp.int32, (1, CH), 1) // HEAD_DIM
    masks = [(lane_head == h).astype(F32).astype(BF16) for h in range(HEADS)]

    def blocks(value):
        return jnp.concatenate([value * m for m in masks], axis=0)

    def side_by_side(value):
        return jnp.concatenate([value[h * 128:(h + 1) * 128, :] for h in range(HEADS)], axis=1)

    def forward(r, n):
        x = jnp.concatenate(
            [u32[pl.ds(2 * n + half, SEQ, stride=4), :] for half in range(2)], axis=1
        )
        hat, scale = standardize(x)
        hat_in[r] = hat
        sc_in[r] = jnp.broadcast_to(scale, (SEQ, 128))
        normed = hat.astype(BF16)
        q = (nn(normed, wq_ref[...]) * HEAD_DIM ** (-0.5)).astype(BF16)
        k = nn(normed, wk_ref[...]).astype(BF16)
        v = nn(normed, wv_ref[...]).astype(BF16)
        g = jax.nn.sigmoid(nn(normed, wg_ref[...]) + shift_ref[...])
        q_all[r] = q
        k_all[r] = k
        v_all[r] = v
        gate[r] = g
        scores = nt(blocks(q), k)
        e = jnp.exp(scores - jnp.max(scores, axis=-1, keepdims=True))
        w = e * (1.0 / jnp.sum(e, axis=-1, keepdims=True))
        w_all[r] = w
        a = nn(side_by_side(w.astype(BF16)), blocks(v))
        att[r] = a
        gated = (a * g).astype(BF16)
        upd = (x + nn(gated, wo_ref[...])).astype(BF16).astype(F32)
        hat, scale = standardize(upd)
        hat_mid[r] = hat
        sc_mid[r] = jnp.broadcast_to(scale, (SEQ, 128))
        normed = hat.astype(BF16)
        nmid[r] = normed
        factors = nt(wf_ref[...], normed).astype(BF16)
        return factors

    def forward_pair(p, carry):
        drain(xr.at[p], N_DAP, recv.at[p])
        u32[0:512, :] = xr[p].astype(F32).reshape(512, 128)
        both = [forward(2 * p + n, n) for n in range(2)]
        ls[p] = jnp.concatenate([factors[0:32, :] for factors in both], axis=0)
        rs[p] = jnp.concatenate([factors[32:64, :] for factors in both], axis=0)
        push_z(rs.at[p], rg.at[p], 15 + p, False)
        push_wide(ls.at[p], lg.at[p], 11 + p, False)
        lg[p, wide] = ls[p]
        rg[p, along] = rs[p]
        return carry

    lax.fori_loop(0, 2, forward_pair, 0)

    push_all(us, ur, 2)

    drain(gr, N_WIDE, recv.at[8])
    t32[...] = gr[...].astype(F32).reshape(2048, 128)

    for jn in range(32):
        from_j = (jn // 16 * 2 + jn % 2) * 8 + jn % 16 // 2
        part = jnp.concatenate(
            [t32[pl.ds(r * 32 + from_j, 16, stride=128), :] for r in range(RES)], axis=0
        ).astype(BF16)
        g2[jn, 0:64, 0:128] = part
        g2[jn, 64:128, 128:256] = part

    for at in range(8):
        res = nt(w2[...], g2[at * 4:at * 4 + 4].reshape(512, 256)).astype(BF16)
        for jj in range(4):
            for c_hi in range(16):
                y[at * 4 + jj, :, c_hi * 128:(c_hi + 1) * 128] = res[
                    c_hi * 32:(c_hi + 1) * 32, jj * 128:(jj + 1) * 128
                ]
    for r in range(RES):
        w_t[r] = w_all[r].astype(BF16).T

    for p in range(2):
        drain(lg.at[p], N_WIDE, recv.at[11 + p])
    t32[...] = lg[...].astype(F32).reshape(2048, 128)
    for c in range(32):
        part = jnp.concatenate(
            [
                t32[pl.ds((r // 2) * 1024 + (r % 2) * 32 + c, 16, stride=64), :]
                for r in range(RES)
            ],
            axis=0,
        )
        lp[c * 64:(c + 1) * 64, :] = part.astype(BF16)

    for p in range(2):
        res = nn(y[p * 16:(p + 1) * 16].reshape(512, 2048), lp[...]).astype(BF16)
        grs[p] = res.reshape(8, 64, 128)
    for p in range(2):
        grr[p, along] = grs[p, along]
        push_z(grs.at[p], grr.at[p], 19 + p, True)

    for p in range(2):
        drain(rg.at[p], N_Z, recv.at[15 + p])
    rg_t = rg[...].reshape(1024, 128).astype(F32).T.astype(BF16)
    for at in range(4):
        res = nn(rg_t, y[:, :, at * 512:(at + 1) * 512].reshape(1024, 512))
        t32[at * 512:(at + 1) * 512, :] = res.T
    for m in range(16):
        gls[m % 2, m // 2] = jnp.concatenate(
            [t32[pl.ds(m + 16 * r, 32, stride=64), :] for r in range(RES)], axis=0
        ).astype(BF16)
    pltpu.make_async_remote_copy(
        src_ref=gls.at[1 - core_here],
        dst_ref=glx,
        send_sem=send.at[24],
        recv_sem=recv.at[24],
        device_id=(sibling, sample),
        device_id_type=MESH,
    ).start()

    for group in range(4):
        if group == 2:
            pltpu.make_async_copy(glx, glx, recv.at[24]).wait()
            glo[...] = (gls[core_here].astype(F32) + glx[...].astype(F32)).astype(BF16)
            glr[level] = glo[level]
            push(level_group, sample, glo, glr, send.at[23], recv.at[23], True)
        res = nt(rg[...].reshape(1024, 128), lp[group * 512:(group + 1) * 512, :]).astype(BF16)
        for jn in range(32):
            for cc in range(4):
                c_hi = group * 4 + cc
                xp[c_hi * 32:(c_hi + 1) * 32, jn * 128:(jn + 1) * 128] = res[
                    jn * 32:(jn + 1) * 32, cc * 128:(cc + 1) * 128
                ]
    pacc[...] = nn(xp[...], g2[...].reshape(4096, 256))

    for m in range(16):
        part = pacc[m * 32:(m + 1) * 32, :] * (1.0 / SEQ)
        ps[m] = jnp.concatenate([part[:, 0:128], part[:, 128:256]], axis=0).astype(BF16)
    pr[wide] = ps[wide]
    push_wide(ps, pr, 27, True)

    for p in range(2):
        drain(grr.at[p], N_Z, recv.at[19 + p])
    right_sum = jnp.sum(grr[...].astype(F32), axis=1).reshape(128, SEQ)
    drain(glr, N_Z, recv.at[23])
    left_sum = jnp.sum(glr[...].astype(F32), axis=0)
    owg = jnp.zeros((64, CH), F32)
    for r in range(RES):
        both = jnp.concatenate(
            [left_sum[r * 32:(r + 1) * 32, :], right_sum[r * 32:(r + 1) * 32, :]], axis=0
        )
        owg = owg + nn(both.astype(BF16), nmid[r])
        dcat[r] = both.T.astype(BF16)

    for m in range(16):
        half = m // 8
        qs[m] = jnp.concatenate(
            [
                owg[(m % 8) * 8:(m % 8) * 8 + 8, half * 128:(half + 1) * 128],
                jnp.zeros((8, 128), F32),
            ],
            axis=0,
        ).astype(BF16)
    qr[wide] = qs[wide]
    push_wide(qs, qr, 38, True)

    drain(ur, N_DAP, recv.at[2])
    t32[1024:2048, :] = ur[...].astype(F32).reshape(1024, 128)

    def backward(r, n):
        grad = nn(dcat[r], wf_ref[...]).astype(BF16).astype(F32)
        dmid = standardize_back(grad, hat_mid[r], sc_mid[r][:, 0:1]).astype(BF16).astype(F32)
        arriving = jnp.concatenate(
            [t32[pl.ds(1024 + 2 * r + half, SEQ, stride=8), :] for half in range(2)], axis=1
        )
        gm16 = (arriving + dmid).astype(BF16)
        gm = gm16.astype(F32)
        dgated = nt(gm16, wo_ref[...]).astype(BF16).astype(F32)
        g = gate[r]
        datt = blocks((dgated * g).astype(BF16))
        dpre = (dgated * att[r] * g * (1.0 - g)).astype(BF16)
        w = w_all[r]
        dw = nt(datt, v_all[r])
        ds = w * (dw - jnp.sum(w * dw, axis=-1, keepdims=True))
        dq = nn(side_by_side(ds.astype(BF16)), blocks(k_all[r])).astype(BF16)
        dq = (dq.astype(F32) * HEAD_DIM ** (-0.5)).astype(BF16)
        dk = nn(ds.T.astype(BF16), blocks(q_all[r])).astype(BF16)
        dv = nn(w_t[r], datt).astype(BF16)
        dnorm = (
            nt(dq, wq_ref[...]) + nt(dk, wk_ref[...]) + nt(dv, wv_ref[...]) + nt(dpre, wg_ref[...])
        ).astype(BF16).astype(F32)
        dx = standardize_back(dnorm, hat_in[r], sc_in[r][:, 0:1]).astype(BF16).astype(F32)
        total = gm + dx
        for half in range(2):
            u32[pl.ds(2 * r + half, SEQ, stride=8), :] = total[:, half * 128:(half + 1) * 128]

    def send_pair(p):
        if p == 1:
            os[...] = u32[...].reshape(N_DAP, 8, 128).astype(BF16)
            orr[me] = os[me]
            push_all(os, orr, 3)

    for n in range(2):
        backward(n, n)

    drain(pr, N_WIDE, recv.at[27])
    zs[...] = jnp.sum(pr[...].astype(F32), axis=0).astype(BF16)
    zr[along] = zs[...]
    push_z(zs, zr, 28, False)
    send_pair(0)

    for n in range(2):
        backward(2 + n, n)
    drain(qr, N_WIDE, recv.at[38])
    zq[...] = jnp.sum(qr[...].astype(F32), axis=0).astype(BF16)
    zqr[along] = zq[...]
    push_z(zq, zqr, 39, False)
    send_pair(1)

    drain(zr, N_Z, recv.at[28])
    fs[...] = jnp.sum(zr[...].astype(F32), axis=0).astype(BF16)
    fr[wide] = fs[...]
    push_wide(fs, fr, 29, False)
    drain(zqr, N_Z, recv.at[39])
    fq[...] = jnp.sum(zqr[...].astype(F32), axis=0).astype(BF16)
    fqr[wide] = fq[...]
    push_wide(fq, fqr, 40, False)

    rfg_ref[...] = right_sum
    drain(xr.at[0], N_DAP, send.at[0])
    drain(xr.at[1], N_DAP, send.at[1])
    drain(ur, N_DAP, send.at[2])
    for p in range(2):
        drain(lg.at[p], N_WIDE, send.at[11 + p])
        drain(rg.at[p], N_Z, send.at[15 + p])
        drain(grr.at[p], N_Z, send.at[19 + p])
    drain(glr, N_Z, send.at[23])
    pltpu.make_async_copy(glx, glx, send.at[24]).wait()
    drain(gr, N_WIDE, send.at[8])
    drain(pr, N_WIDE, send.at[27])
    drain(qr, N_WIDE, send.at[38])
    drain(zr, N_Z, send.at[28])
    drain(zqr, N_Z, send.at[39])

    drain(fr, N_WIDE, recv.at[29])
    drain(fqr, N_WIDE, recv.at[40])
    halves = []
    for m in range(16):
        pwg_ref[m * 64:(m + 1) * 64, :] = fr[m].astype(F32)
        halves.append(fqr[m].astype(F32)[0:8, :])
    owg_ref[...] = jnp.concatenate(
        [jnp.concatenate(halves[0:8], axis=0), jnp.concatenate(halves[8:16], axis=0)], axis=1
    )
    drain(fr, N_WIDE, send.at[29])
    drain(fqr, N_WIDE, send.at[40])

    drain(orr, N_DAP, recv.at[3])
    u32[...] = orr[...].astype(F32).reshape(1024, 128)
    out_ref[:, 0:128] = u32[pl.ds(0, 512, stride=2), :].astype(BF16)
    out_ref[:, 128:256] = u32[pl.ds(1, 512, stride=2), :].astype(BF16)
    drain(orr, N_DAP, send.at[3])


def settle(*refs):
    found, results, sems = refs[0:4], refs[4:8], refs[8]
    copies = [pltpu.make_async_copy(found[n], results[n], sems.at[n]) for n in range(4)]
    for copy in copies:
        copy.start()
    for copy in copies:
        copy.wait()


SCRATCH = (
    [((512, CH), BF16)]
    + [((CH, CH), BF16)] * 4
    + [((1, CH), F32), ((CH, CH), BF16), ((64, CH), BF16), ((1024, 128), BF16)]
    + [((512, CH), BF16), ((2048, 128), BF16)]
    + [((2, N_DAP, 4, 128), BF16)] * 2
    + [((N_DAP, 8, 128), BF16)] * 2
    + [((16, 128, 128), BF16)] * 2
    + [((2048, 128), F32), ((1024, 128), F32)]
    + [((RES, SEQ, CH), F32)]
    + [((RES, SEQ, 128), F32)]
    + [((RES, SEQ, CH), F32)] * 2
    + [((RES, SEQ, CH), BF16)] * 3
    + [((RES, HEADS * SEQ, SEQ), F32)]
    + [((RES, SEQ, CH), BF16)]
    + [((RES, SEQ, CH), F32)]
    + [((RES, SEQ, 128), F32)]
    + [((2, 64, 128), BF16), ((2, 16, 64, 128), BF16)]
    + [((2, 64, 128), BF16), ((2, 8, 64, 128), BF16)]
    + [((2048, 128), BF16)]
    + [((32, 128, 256), BF16)]
    + [((512, 256), BF16)]
    + [((32, 32, 2048), BF16)]
    + [((512, 4096), BF16)]
    + [((512, 256), F32)]
    + [((2, 8, 128, 128), BF16)]
    + [((8, 128, 128), BF16)] * 3
    + [((2, 8, 64, 128), BF16)] * 2
    + [((RES, SEQ, 64), BF16)]
    + [((16, 64, 128), BF16)] * 2
    + [((16, 16, 128), BF16)] * 2
    + [((64, 128), BF16), ((8, 64, 128), BF16)]
    + [((16, 128), BF16), ((8, 16, 128), BF16)]
    + [((64, 128), BF16), ((16, 64, 128), BF16)]
    + [((16, 128), BF16), ((16, 16, 128), BF16)]
    + [((N_DAP, 8, 128), BF16)] * 2
    + [((RES, SEQ, HEADS * SEQ), BF16)]
)
SEMAPHORES = 41


def body(
    aligned_rows,
    asking_projection,
    lookup_projection,
    content_projection,
    sigmoid_projection,
    sigmoid_shift,
    result_projection,
    tensor_mean_projections,
    twofold_projection,
    refreshed_rows_adjoint,
    twofold_change_adjoint,
):
    whole = pl.BlockSpec(memory_space=pltpu.VMEM)
    anywhere = pl.BlockSpec(memory_space=pl.ANY)
    results = (
        jax.ShapeDtypeStruct((512, CH), BF16),
        jax.ShapeDtypeStruct((1024, 128), F32),
        jax.ShapeDtypeStruct((64, CH), F32),
        jax.ShapeDtypeStruct((128, SEQ), F32),
    )
    found = pl.pallas_call(
        kernel,
        out_shape=tuple(pltpu.VMEM(result.shape, result.dtype) for result in results),
        in_specs=[anywhere] * 11,
        out_specs=(whole,) * 4,
        scratch_shapes=[pltpu.VMEM(shape, kind) for shape, kind in SCRATCH]
        + [pltpu.SemaphoreType.DMA((SEMAPHORES,)), pltpu.SemaphoreType.DMA((SEMAPHORES,))]
        + [pltpu.SemaphoreType.DMA((11,))],
        compiler_params=pltpu.CompilerParams(
            collective_id=0, has_side_effects=True, vmem_limit_bytes=56 * 2**20
        ),
        name="evoformer_backward",
    )(
        aligned_rows.reshape(512, CH),
        asking_projection,
        lookup_projection,
        content_projection,
        sigmoid_projection,
        sigmoid_shift.reshape(1, CH),
        result_projection,
        tensor_mean_projections.T,
        twofold_projection,
        refreshed_rows_adjoint.reshape(512, CH),
        twofold_change_adjoint.reshape(2048, 128),
    )
    out, pwg, owg, rfg = pl.pallas_call(
        settle,
        out_shape=results,
        in_specs=[anywhere] * 4,
        out_specs=(anywhere,) * 4,
        scratch_shapes=[pltpu.SemaphoreType.DMA((4,))],
        name="settle",
    )(*[pltpu.with_memory_space_constraint(array, pltpu.VMEM) for array in found])
    return (
        out.reshape(1, 512, CH),
        pwg,
        owg.T,
        rfg.reshape(RES, 32, SEQ).transpose(2, 0, 1),
    )


def solution(mesh):
    split = P(("dp", "dap"), None, None)
    in_specs = (split,) + (P(),) * 8 + (split, split)
    out_specs = (split, P("dp", None), P("dp", None), P("dp", "dap", None))
    return jax.shard_map(body, mesh=mesh, in_specs=in_specs, out_specs=out_specs, check_vma=False)
```
